512 devices in a mesh: box: 128 (over y, z, core), sub: 4 (over x).
Axes of the slice: x: 4, y: 4, z: 16, core: 2. Of those that a mesh axis runs over, the one named last changes fastest.
Arguments:
- charges: bfloat16 [24576, 1024], P(('box', 'sub')), may hold values from -6 to 6
- coords: float32 [24576, 192], P(('box', 'sub')), may hold values from 0 to 2
- basis: bfloat16 [24576, 4096], P(('box', 'sub')), may hold values from -0.75 to 0.75
- transfer: bfloat16 [24576, 4096], P(('box', 'sub')), may hold values from -0.5 to 0.5
- leaf_table: bfloat16 [96, 4096], replicated, may hold values from -0.078125 to 0.078125
- upper_table: bfloat16 [64, 4096], replicated, may hold values from -0.09375 to 0.09375
- near_ids: int32 [24576, 27], P(('box', 'sub')), may hold values from 0 to 24575, as said below
- near_count: int32 [24576], P(('box', 'sub')), may hold values from 1 to 27, as said below
- leaf_ids: int32 [24576, 96], P(('box', 'sub')), may hold values from 0 to 24575, as said below
- parent_ids: int32 [3072, 64], P(('box', 'sub')), may hold values from 0 to 3071, as said below
Outputs:
- potential: float32 [24576, 1024], P(('box', 'sub'))
The draws below stay inside these ranges and needn't reach their ends.
Inputs may be any that keep to these rules, and one draw needn't show every extreme that they name: `near_ids`: A device holds 48 consecutive leaf boxes. Entry 0 of a list is the box itself; the others are distinct boxes other than itself on the same device or the devices just before and after it. Only the first near_count entries of a list are used; the first box of every device uses all 27. `leaf_ids`: sources are boxes other than the box itself on the same device or the devices just before and after it; they may repeat. `parent_ids`: parents are numbered in Morton order, 24 consecutive ones to each index of box. Sources are parents other than the parent itself in the same group or the groups just before and after it; they may repeat.
All inputs are finite; a program needn't handle non-finite values.
Results may differ from the reference program's by a relative error of at most 0.011.
Values may be sent and summed in bfloat16 or wider, within the bound.
No kernel may reach another device: no remote copies, remote signals or barrier semaphores. Data moves between devices by JAX's collectives and lax.ppermute only.
A program may use at most 64 MiB of HBM per device.

```python
import math
import jax
import jax.numpy as jnp
from jax import lax

POINTS = 64
RANK = 64
RHS = 16
NEAR = 27
LEAF_OFFSETS = 96
UPPER_OFFSETS = 64
LEAF_DEV = 48
LEAVES = 24576
PARENTS = 3072
GROUP_PARENTS = 24


def window_sources(key, total, per_group, count):
    boxes = jnp.arange(total, dtype=jnp.int32)
    groups = boxes // per_group
    lowest = jnp.maximum(groups - 1, 0) * per_group
    highest = jnp.minimum(groups + 2, total // per_group) * per_group
    picked = jax.random.randint(key, (total, count), 0, (highest - lowest - 1)[:, None])
    sources = lowest[:, None] + picked
    return (sources + (sources >= boxes[:, None]).astype(jnp.int32)).astype(jnp.int32)


def draw_near_ids(key, part):
    key = jax.random.fold_in(key, 11)
    boxes = jnp.arange(LEAVES, dtype=jnp.int32)
    lowest = (boxes // LEAF_DEV - 1) * LEAF_DEV
    spread = jnp.arange(3 * LEAF_DEV, dtype=jnp.int32)
    candidate = lowest[:, None] + spread[None, :]
    usable = (candidate >= 0) & (candidate < LEAVES) & (candidate != boxes[:, None])
    scores = jax.random.randint(key, (LEAVES, 3 * LEAF_DEV), 0, 1 << 20) * (3 * LEAF_DEV) + spread[None, :]
    scores = jnp.where(usable, scores, -1)
    _, picked = lax.top_k(scores, NEAR - 1)
    others = lowest[:, None] + picked.astype(jnp.int32)
    return jnp.concatenate([boxes[:, None], others], axis=1).astype(jnp.int32)


def draw_near_count(key, part):
    key = jax.random.fold_in(key, 14)
    first_key, second_key = jax.random.split(key)
    device_most = jax.random.randint(first_key, (LEAVES // LEAF_DEV,), NEAR // 3, NEAR + 1)
    most = jnp.repeat(device_most, LEAF_DEV)
    counts = 1 + jax.random.randint(second_key, (LEAVES,), 0, most)
    leading = jnp.arange(LEAVES, dtype=jnp.int32) % LEAF_DEV == 0
    return jnp.where(leading, NEAR, counts).astype(jnp.int32)


def draw_leaf_ids(key, part):
    key = jax.random.fold_in(key, 12)
    return window_sources(key, LEAVES, LEAF_DEV, LEAF_OFFSETS)


def draw_parent_ids(key, part):
    key = jax.random.fold_in(key, 13)
    return window_sources(key, PARENTS, GROUP_PARENTS, UPPER_OFFSETS)


def steps_of(key, extent, cuts, smallest, top_value):
    def one(position, shards_of):
        draws = jax.random.uniform(jax.random.fold_in(jax.random.fold_in(key, 6), position), (shards_of,), jnp.float32, smallest / len(cuts), top_value / len(cuts))
        return jnp.repeat(jnp.exp(draws), extent[position] // shards_of).reshape((-1,) + (1,) * (len(extent) - position - 1))

    gain = one(*cuts[0])
    for cut in cuts[1:]:
        gain = gain * one(*cut)
    return gain


def noise(stream_key, dims, width, limit, pieces=(), kind=jnp.bfloat16):
    values = width * jax.random.normal(stream_key, dims, jnp.float32)
    if pieces:
        values = values * steps_of(stream_key, dims, pieces, -0.22, 0.18)
    return jnp.clip(values, -limit, limit).astype(kind)


def setup_inputs(seed: int = 0) -> dict:
    splits = jax.random.split(jax.random.key(seed), 11)
    charges = noise(splits[0], (LEAVES, POINTS * RHS), 1.0, 6.0, ((0, 512),))
    coords = jnp.clip(2.0 * jax.random.uniform(splits[1], (LEAVES, 3 * POINTS), jnp.float32) ** steps_of(splits[1], (LEAVES, 3 * POINTS), ((0, 512),), -0.2, 0.2), 0.0, 2.0)
    basis = noise(splits[2], (LEAVES, POINTS * RANK), POINTS ** -0.5, 0.75, ((0, 512),))
    transfer = noise(splits[3], (LEAVES, RANK * RANK), (2 * RANK) ** -0.5, 0.5, ((0, 512),))
    leaf_table = noise(splits[4], (LEAF_OFFSETS, RANK * RANK), (RANK * LEAF_OFFSETS) ** -0.5, 0.078125)
    upper_table = noise(splits[5], (UPPER_OFFSETS, RANK * RANK), (RANK * UPPER_OFFSETS) ** -0.5, 0.09375)
    near_ids = draw_near_ids(jax.random.fold_in(splits[10], 71), 0)
    near_count = draw_near_count(jax.random.fold_in(splits[10], 71), 0)
    leaf_ids = draw_leaf_ids(jax.random.fold_in(splits[10], 71), 0)
    parent_ids = draw_parent_ids(jax.random.fold_in(splits[10], 71), 0)
    return {"charges": charges, "coords": coords, "basis": basis, "transfer": transfer, "leaf_table": leaf_table, "upper_table": upper_table, "near_ids": near_ids, "near_count": near_count, "leaf_ids": leaf_ids, "parent_ids": parent_ids}


SOFT = 0.05
QUARTER = 0.25 / math.pi

def reference(charges, coords, basis, transfer, leaf_table, upper_table, near_ids, near_count, leaf_ids, parent_ids):
    leaves = charges.shape[0]
    parents = leaves // 8
    charge_cube = charges.reshape(leaves, POINTS, RHS)
    point_cube = coords.reshape(leaves, 3, POINTS)
    bases = basis.reshape(leaves, POINTS, RANK).astype(jnp.float32)
    shifts = transfer.reshape(leaves, RANK, RANK).astype(jnp.float32)
    skeleton = jnp.einsum('bpk,bpr->bkr', bases, charge_cube.astype(jnp.float32)).astype(jnp.bfloat16)
    lifted = jnp.einsum('bjk,bjr->bkr', shifts, skeleton.astype(jnp.float32))
    upper_skeleton = lax.optimization_barrier(jnp.sum(lifted.reshape(parents, 8, RANK, RHS), axis=1)).astype(jnp.bfloat16)
    leaf_ops = leaf_table.reshape(LEAF_OFFSETS, RANK, RANK).astype(jnp.float32)
    upper_ops = upper_table.reshape(UPPER_OFFSETS, RANK, RANK).astype(jnp.float32)

    def leaf_far(source_ids):
        sources = skeleton[source_ids].astype(jnp.float32)
        return jnp.einsum('okl,bolr->bkr', leaf_ops, sources)
    local_field = lax.map(leaf_far, leaf_ids.reshape(leaves // LEAF_DEV, LEAF_DEV, LEAF_OFFSETS)).reshape(leaves, RANK, RHS)

    def upper_far(source_ids):
        sources = upper_skeleton[source_ids].astype(jnp.float32)
        return jnp.einsum('okl,bolr->bkr', upper_ops, sources)
    upper_field = lax.map(upper_far, parent_ids.reshape(parents // GROUP_PARENTS, GROUP_PARENTS, UPPER_OFFSETS))
    upper_field = upper_field.reshape(parents, RANK, RHS).astype(jnp.bfloat16)
    descended = jnp.einsum('bjk,bkr->bjr', shifts, jnp.repeat(upper_field, 8, axis=0).astype(jnp.float32))
    field = (local_field + descended).astype(jnp.bfloat16)
    far_field = jnp.einsum('bpk,bkr->bpr', bases, field.astype(jnp.float32))

    def near_part(block_data):
        source_ids, counts, targets = block_data
        source_q = charge_cube[source_ids].astype(jnp.float32)
        source_x = point_cube[source_ids]
        distance = None
        for axis_index in range(3):
            separation = targets[:, None, axis_index, :, None] - source_x[:, :, axis_index, None, :]
            squared = separation * separation
            distance = squared if distance is None else distance + squared
        active_slot = jnp.arange(NEAR, dtype=jnp.int32)[None, :] < counts[:, None]
        kernel = jnp.where(active_slot[:, :, None, None], QUARTER / jnp.sqrt(distance + SOFT), 0.0).astype(jnp.bfloat16)
        return jnp.einsum('bnij,bnjr->bir', kernel.astype(jnp.float32), source_q)
    near_field = lax.map(near_part, (near_ids.reshape(-1, LEAF_DEV, NEAR), near_count.reshape(-1, LEAF_DEV), point_cube.reshape(-1, LEAF_DEV, 3, POINTS)))
    near_field = near_field.reshape(leaves, POINTS, RHS)
    return (near_field + far_field).reshape(leaves, POINTS * RHS)
```

```python
import functools
import math

import jax
import jax.numpy as jnp
from jax import lax
from jax.experimental import pallas as pl
from jax.experimental.pallas import tpu as pltpu
from jax.sharding import PartitionSpec as P

SOFT = 0.05
SCALE = 16.0 * math.pi * math.pi
F32 = jnp.float32
BF16 = jnp.bfloat16
BOXES = 48
PAIRS = BOXES // 2
NEAR = 27
OFFSETS = 96
UPPER = 64
PARENTS = 6
S_ROWS = PAIRS * 16
U_ROWS = PARENTS // 2 * 16
VMEM_LIMIT = 48 * 1024 * 1024


def nn(a, b):
    return lax.dot_general(a, b, (((1,), (0,)), ((), ())), preferred_element_type=F32)


def nt(a, b):
    return lax.dot_general(a, b, (((1,), (1,)), ((), ())), preferred_element_type=F32)


def iota(shape, dim):
    return lax.broadcasted_iota(jnp.int32, shape, dim)


def onehot(cond):
    return jnp.where(cond, 1.0, 0.0).astype(BF16)


def half_swap(x):
    return pltpu.roll(x, 64, 1)


def skeleton_kernel(q_ref, v_ref, e_ref, su_ref, xv_ref, xe_ref, qs, vs, es):
    for i in range(8):
        qs[i * BOXES : (i + 1) * BOXES] = q_ref[:, i * 128 : (i + 1) * 128].astype(F32)
    for t in range(32):
        vs[t * BOXES : (t + 1) * BOXES] = v_ref[:, t * 128 : (t + 1) * 128].astype(F32)
    for t in range(32):
        es[t * BOXES : (t + 1) * BOXES] = e_ref[:, t * 128 : (t + 1) * 128].astype(F32)
    row = iota((32, 128), 0)
    lane = iota((32, 128), 1)
    pick = onehot((lane % 32) == row)
    lane8 = iota((8, 128), 1) // 32
    lane16 = iota((16, 128), 1)
    low = lane16 < 64
    group = lane // 32
    for g in range(BOXES // 4):
        parts = []
        for c in range(4):
            b = g * 4 + c
            rows = qs[pl.ds(b, 8, stride=BOXES), :]
            parts += [jnp.where(lane8 == m, rows, 0.0) for m in range(4)]
        weights = jnp.concatenate(parts, axis=0).astype(BF16)
        q2 = nt(pick, weights)
        lhs = jnp.concatenate([jnp.where(group == c, q2, 0.0) for c in range(4)], axis=0).astype(BF16)
        vb = []
        for c in range(4):
            b = g * 4 + c
            vb += [vs[pl.ds(m * BOXES + b, 8, stride=4 * BOXES), :] for m in range(4)]
        xv = jnp.concatenate(vb, axis=0).astype(BF16)
        xv_ref[g * 128 : (g + 1) * 128] = xv
        z = nn(lhs, xv)
        for u in range(2):
            o = u * 64
            even = z[o : o + 16] + half_swap(z[o + 16 : o + 32])
            odd = half_swap(z[o + 32 : o + 48]) + z[o + 48 : o + 64]
            r = (g * 2 + u) * 16
            su_ref[r : r + 16] = jnp.where(low, even, odd).astype(BF16)
    prow = iota((256, 256), 0)
    pcol = iota((256, 256), 1)
    spread = onehot(
        ((prow // 64) == ((pcol % 128) // 32)) & ((prow % 64) == 2 * (pcol % 32) + pcol // 128)
    )
    lifted = []
    for p in range(PARENTS):
        lhs = []
        xe = []
        for h in range(2):
            g = p * 2 + h
            s = su_ref[g * 32 : g * 32 + 32]
            wide = jnp.concatenate([s[:16], s[16:]], axis=1)
            moved = nn(wide, spread)
            lhs.append(jnp.concatenate([moved[:, :128], moved[:, 128:]], axis=0))
            for c in range(4):
                xe.append(es[pl.ds(g * 4 + c, 32, stride=BOXES), :])
        lhs = jnp.concatenate(lhs, axis=1).astype(BF16)
        xe = jnp.concatenate(xe, axis=0).astype(BF16)
        xe_ref[p * 256 : (p + 1) * 256] = xe
        z = nn(lhs, xe)
        if p % 2 == 0:
            lifted = z[:16] + half_swap(z[16:])
        else:
            other = half_swap(z[:16]) + z[16:]
            r = S_ROWS + (p // 2) * 16
            su_ref[r : r + 16] = jnp.where(low, lifted, other).astype(BF16)


def pack_kernel(q_ref, x_ref, out_ref, qs):
    for i in range(8):
        qs[i * BOXES : (i + 1) * BOXES] = q_ref[:, i * 128 : (i + 1) * 128].astype(F32)
    own = iota((8, 128), 0) == iota((8, 128), 1) // 16
    pick = onehot((iota((16, 128), 1) % 16) == iota((16, 128), 0))
    for u in range(PAIRS):
        parts = []
        for c in range(2):
            rows = qs[pl.ds(u * 2 + c, 8, stride=BOXES), :]
            for i in range(8):
                parts.append(jnp.where(own, jnp.broadcast_to(rows[i : i + 1], (8, 128)), 0.0))
        weights = jnp.concatenate(parts, axis=0).astype(BF16)
        out_ref[u * 16 : u * 16 + 16] = nt(pick, weights).astype(BF16)
    out_ref[S_ROWS : S_ROWS + BOXES] = x_ref[:, :128].astype(BF16)
    out_ref[S_ROWS + BOXES : S_ROWS + 2 * BOXES] = jnp.concatenate(
        [x_ref[:, 128:], jnp.zeros((BOXES, 64), F32)], axis=1
    ).astype(BF16)


def table_kernel(leaf_ref, upper_ref, wl_ref, wu_ref, ts):
    low = iota((32, 128), 1) < 64
    for ref, out, count in ((leaf_ref, wl_ref, OFFSETS), (upper_ref, wu_ref, UPPER)):
        for t in range(32):
            ts[t * count : (t + 1) * count] = ref[:, t * 128 : (t + 1) * 128].astype(F32)
        for u in range(count // 2):
            first = ts[pl.ds(2 * u, 32, stride=count), :]
            second = ts[pl.ds(2 * u + 1, 32, stride=count), :]
            even = jnp.where(low, first, half_swap(second))
            odd = jnp.where(low, half_swap(first), second)
            out[:, u * 128 : (u + 1) * 128] = jnp.concatenate([even, odd], axis=0).astype(BF16)


def split3(x):
    a = x.astype(BF16).astype(F32)
    rest = x - a
    b = rest.astype(BF16).astype(F32)
    return a, b, rest - b


def dup_matrix():
    r = iota((128, 256), 0)
    c = iota((128, 256), 1)
    return onehot((r // 64 == c // 128) & (r % 64 == c % 64))


def spread_pairs(src_ref, rows, dst_ref, base):
    wide = nn(src_ref[:rows], dup_matrix()).astype(BF16)
    for u in range(rows // 16):
        dst_ref[base + 2 * u] = wide[u * 16 : u * 16 + 16, :128]
        dst_ref[base + 2 * u + 1] = wide[u * 16 : u * 16 + 16, 128:]


STEP = 4


def near_kernel(
    info, ids, counts, own_ref, prev_ref, next_ref, x_ref, out_ref, qt, yt, at, ks, bs, acc, place, sums
):
    first = info[0]
    for side, ref in enumerate((prev_ref, own_ref, next_ref)):
        spread_pairs(ref, S_ROWS, qt, side * BOXES)
    qt[3 * BOXES] = jnp.zeros((16, 128), BF16)
    total = 3 * BOXES
    lanes = iota((BOXES, 128), 1) < 64

    def dup3(xy, z):
        flip = half_swap(xy)
        return jnp.where(lanes, xy, flip), jnp.where(lanes, flip, xy), jnp.where(lanes, z, half_swap(z))

    ones = jnp.ones((BOXES, 128), F32)
    zeros = jnp.zeros((BOXES, 128), F32)
    for side, ref in enumerate((prev_ref, own_ref, next_ref)):
        xy = ref[S_ROWS : S_ROWS + BOXES].astype(F32)
        z = ref[S_ROWS + BOXES : S_ROWS + 2 * BOXES].astype(F32)
        y0, y1, y2 = dup3(xy, z)
        n = split3(SCALE * (y0 * y0 + y1 * y1 + y2 * y2))
        for k, v in enumerate((y0, y0, y0, y1, y1, y1, y2, y2, y2, *n, ones, ones, ones, zeros)):
            bs[k * BOXES : (k + 1) * BOXES] = v
        for b in range(BOXES):
            yt[side * BOXES + b] = bs[pl.ds(b, 16, stride=BOXES), :].astype(BF16)
    yt[total] = onehot(iota((16, 128), 0) >= 12)
    zx = jnp.concatenate([x_ref[:, 128:], jnp.zeros((BOXES, 64), F32)], axis=1)
    x0, x1, x2 = dup3(x_ref[:, :128], zx)
    n = split3(SCALE * (x0 * x0 + x1 * x1 + x2 * x2 + SOFT))
    cols = []
    for x in (x0, x1, x2):
        cols += list(split3((-2.0 * SCALE) * x))
    for k, v in enumerate((*cols, ones, ones, ones, *n, zeros)):
        bs[k * BOXES : (k + 1) * BOXES] = v
    eye = onehot((iota((64, 128), 0) == iota((64, 128), 1)))
    for b in range(BOXES):
        at[b] = nt(eye, bs[pl.ds(b, 16, stride=BOXES), :].astype(BF16)).astype(BF16)
        acc[b] = jnp.zeros((16, 64), F32)
    acc[BOXES] = jnp.zeros((16, 64), F32)
    at[BOXES] = jnp.zeros((64, 16), BF16) + onehot(iota((64, 16), 1) == 12)
    low = iota((16, 128), 1) < 64

    def advance(box, chunk):
        here = jnp.minimum(box, BOXES - 1)
        more = (chunk + 1) * 8 < counts[here]
        return jnp.where(more, box, box + 1), jnp.where(more, chunk + 1, 0)

    def gather(table, sources):
        tiles = [
            jnp.where(low, table[sources[2 * j]], table[sources[2 * j + 1]])
            for j in range(len(sources) // 2)
        ]
        return jnp.concatenate(tiles, axis=1)

    def work(state):
        step, box, chunk = state
        slot = step % 2
        last = 1 - slot
        for j in range(STEP):
            kernel = ks[last, j]
            here = place[last * STEP * 9 + j * 9]
            sources = [place[last * STEP * 9 + j * 9 + 1 + c] for c in range(8)]
            acc[here] += nt(gather(qt, sources), kernel)
        for j in range(STEP):
            target = jnp.minimum(box, BOXES)
            here = jnp.minimum(box, BOXES - 1)
            used = counts[here]
            sources = []
            for c in range(8):
                n = chunk * 8 + c
                g = ids[here, jnp.minimum(n, NEAR - 1)] - first
                sources.append(jnp.where((n < used) & (box < BOXES), g, total))
            place[slot * STEP * 9 + j * 9] = target
            for c in range(8):
                place[slot * STEP * 9 + j * 9 + 1 + c] = sources[c]
            d = nn(at[target], gather(yt, sources))
            ks[slot, j] = lax.rsqrt(d).astype(BF16)
            box, chunk = advance(box, chunk)
        return step + 1, box, chunk

    for j in range(STEP):
        place[STEP * 9 + j * 9] = BOXES
        for c in range(8):
            place[STEP * 9 + j * 9 + 1 + c] = total
        ks[1, j] = jnp.zeros((64, 512), BF16)
    step, _, _ = lax.while_loop(lambda s: s[1] < BOXES, work, (0, 0, 0))
    last = 1 - step % 2
    for j in range(STEP):
        here = place[last * STEP * 9 + j * 9]
        sources = [place[last * STEP * 9 + j * 9 + 1 + c] for c in range(8)]
        acc[here] += nt(gather(qt, sources), ks[last, j])
    lane8 = iota((8, 128), 1) // 16
    for g in range(BOXES // 8):
        rows = jnp.concatenate([acc[g * 8 + c] for c in range(8)], axis=0)
        sums[...] = rows.T
        tiles = [sums[pl.ds(s, 8, stride=8), :] for s in range(8)]
        for c in range(8):
            total_tile = None
            for s in range(8):
                moved = tiles[s] if s == c else pltpu.roll(tiles[s], (16 * (s - c)) % 128, 1)
                total_tile = moved if total_tile is None else jnp.where(lane8 == s, moved, total_tile)
            out_ref[pl.ds(g * 8 + c, 8, stride=BOXES), :] = total_tile


def couple(table, w_ref, ids, base, first, boxes, offsets, low):
    quads = offsets // 4

    def body(k, total):
        rows = []
        for b in range(boxes):
            g = [ids[base + b, k * 4 + j] - first for j in range(4)]
            rows.append(
                jnp.concatenate(
                    [jnp.where(low, table[g[0]], table[g[1]]), jnp.where(low, table[g[2]], table[g[3]])],
                    axis=1,
                )
            )
        lhs = jnp.concatenate(rows, axis=0)
        return total + nt(lhs, w_ref[:, pl.ds(pl.multiple_of(k * 256, 256), 256)])

    return lax.fori_loop(0, quads, body, jnp.zeros((boxes * 16, 64), F32))


GROUP = 16


def field_kernel(
    info, ids, pids, su_ref, rd1_ref, rd2_ref, bp_ref, bm_ref, wl_ref, wu_ref, xv_ref, xe_ref, near_ref,
    out_ref, st, ut, halo, fs, ps,
):
    first = info[0]
    first_parent = info[1]
    sub = info[2]
    low = iota((16, 128), 1) < 64

    @pl.when(sub == 0)
    def _():
        halo[0] = bp_ref[:S_ROWS]
        halo[1] = rd1_ref[:S_ROWS]

    @pl.when(sub == 1)
    def _():
        halo[0] = rd1_ref[:S_ROWS]
        halo[1] = rd2_ref[:S_ROWS]

    @pl.when(sub == 2)
    def _():
        halo[0] = rd2_ref[:S_ROWS]
        halo[1] = rd1_ref[:S_ROWS]

    @pl.when(sub == 3)
    def _():
        halo[0] = rd1_ref[:S_ROWS]
        halo[1] = bm_ref[:S_ROWS]

    spread_pairs(halo.at[0], S_ROWS, st, 0)
    spread_pairs(su_ref, S_ROWS, st, BOXES)
    spread_pairs(halo.at[1], S_ROWS, st, 2 * BOXES)

    def parents(ref, row, group, flip):
        wide = nn(ref[row : row + U_ROWS], dup_matrix()).astype(BF16)
        at = group * 4 * PARENTS + (sub ^ flip) * PARENTS
        for u in range(PARENTS // 2):
            ut[at + 2 * u] = wide[u * 16 : u * 16 + 16, :128]
            ut[at + 2 * u + 1] = wide[u * 16 : u * 16 + 16, 128:]

    for group, ref in ((0, bp_ref), (2, bm_ref)):
        for j, flip in enumerate((3, 2, 0, 1)):
            parents(ref, S_ROWS + j * U_ROWS, group, flip)
    parents(su_ref, S_ROWS, 1, 0)
    parents(rd1_ref, S_ROWS, 1, 1)
    parents(rd2_ref, S_ROWS, 1, 3)
    parents(rd2_ref, S_ROWS + U_ROWS, 1, 2)

    upper = couple(ut, wu_ref, pids, 0, first_parent, PARENTS, UPPER, low)
    r64 = iota((64, 128), 0)
    c64 = iota((64, 128), 1)
    natural = onehot((c64 % 64) == 2 * (r64 % 32) + r64 // 32)
    upper2 = nn(upper.astype(BF16), natural)
    lane16 = iota((16, 128), 1)
    for p in range(PARENTS):
        u = upper2[p * 16 : p * 16 + 16]
        lhs = jnp.concatenate([jnp.where(low, u, 0.0), jnp.where(low, 0.0, u)], axis=0).astype(BF16)
        down = nt(lhs, xe_ref[p * 256 : (p + 1) * 256])
        for c in range(8):
            tile = down[:, (c // 4) * 128 : (c // 4) * 128 + 128]
            at = (c % 4) * 32
            a = tile[:16] if at == 0 else pltpu.roll(tile[:16], 128 - at, 1)
            b = tile[16:] if at == 32 else pltpu.roll(tile[16:], (160 - at) % 128, 1)
            fs[(p * 8 + c) * 16 : (p * 8 + c + 1) * 16] = jnp.where(lane16 < 32, a, b)
    lane8 = iota((8, 128), 1) // 32
    low64 = iota((16, 128), 1) < 64
    for h in range(BOXES // GROUP):
        part = couple(st, wl_ref, ids, h * GROUP, first, GROUP, OFFSETS, low)
        field = (part + fs[h * GROUP * 16 : (h + 1) * GROUP * 16, :64]).astype(BF16)
        wide = nn(field, natural)
        for q in range(GROUP // 4):
            parts = []
            for c in range(4):
                f = wide[(q * 4 + c) * 16 : (q * 4 + c + 1) * 16]
                parts += [jnp.where(low64, f, 0.0), jnp.where(low64, 0.0, f)]
            weights = jnp.concatenate(parts, axis=0).astype(BF16)
            g = h * (GROUP // 4) + q
            far = nt(xv_ref[g * 128 : (g + 1) * 128], weights)
            for c in range(4):
                tile = None
                for m in range(4):
                    piece = far[c * 32 + m * 8 : c * 32 + m * 8 + 8]
                    if m != c:
                        piece = pltpu.roll(piece, (32 * (m - c)) % 128, 1)
                    tile = piece if tile is None else jnp.where(lane8 == m, piece, tile)
                rows = pl.ds(g * 4 + c, 8, stride=BOXES)
                ps[rows, :] = tile
    for i in range(8):
        rows = slice(i * BOXES, (i + 1) * BOXES)
        out_ref[:, i * 128 : (i + 1) * 128] = near_ref[rows] + ps[rows]


VM = pl.BlockSpec(memory_space=pltpu.VMEM)
SM = pl.BlockSpec(memory_space=pltpu.SMEM)


def params():
    return pltpu.CompilerParams(vmem_limit_bytes=VMEM_LIMIT)


def run_skeleton(charges, basis, transfer):
    return pl.pallas_call(
        skeleton_kernel,
        out_shape=(
            jax.ShapeDtypeStruct((S_ROWS + U_ROWS, 128), BF16),
            jax.ShapeDtypeStruct((BOXES * 32, 128), BF16),
            jax.ShapeDtypeStruct((BOXES * 32, 128), BF16),
        ),
        in_specs=[VM] * 3,
        out_specs=(VM,) * 3,
        scratch_shapes=[
            pltpu.VMEM((8 * BOXES, 128), F32),
            pltpu.VMEM((32 * BOXES, 128), F32),
            pltpu.VMEM((32 * BOXES, 128), F32),
        ],
        compiler_params=params(),
        name="skeleton",
    )(charges, basis, transfer)


def run_pack(charges, coords):
    return pl.pallas_call(
        pack_kernel,
        out_shape=jax.ShapeDtypeStruct((S_ROWS + 2 * BOXES, 128), BF16),
        in_specs=[VM] * 2,
        out_specs=VM,
        scratch_shapes=[pltpu.VMEM((8 * BOXES, 128), F32)],
        compiler_params=params(),
        name="pack",
    )(charges, coords)


def run_tables(leaf_table, upper_table):
    return pl.pallas_call(
        table_kernel,
        out_shape=(
            jax.ShapeDtypeStruct((64, OFFSETS * 64), BF16),
            jax.ShapeDtypeStruct((64, UPPER * 64), BF16),
        ),
        in_specs=[VM] * 2,
        out_specs=(VM,) * 2,
        scratch_shapes=[pltpu.VMEM((32 * OFFSETS, 128), F32)],
        compiler_params=params(),
        name="tables",
    )(leaf_table, upper_table)


def run_near(info, near_ids, near_count, own, before, after, coords):
    return pl.pallas_call(
        near_kernel,
        out_shape=jax.ShapeDtypeStruct((8 * BOXES, 128), F32),
        in_specs=[SM] * 3 + [VM] * 4,
        out_specs=VM,
        scratch_shapes=[
            pltpu.VMEM((3 * BOXES + 1, 16, 128), BF16),
            pltpu.VMEM((3 * BOXES + 1, 16, 128), BF16),
            pltpu.VMEM((BOXES + 1, 64, 16), BF16),
            pltpu.VMEM((2, STEP, 64, 512), BF16),
            pltpu.VMEM((16 * BOXES, 128), F32),
            pltpu.VMEM((BOXES + 1, 16, 64), F32),
            pltpu.SMEM((2 * STEP * 9,), jnp.int32),
            pltpu.VMEM((64, 128), F32),
        ],
        compiler_params=params(),
        name="near",
    )(info, near_ids, near_count, own, before, after, coords)


def run_field(info, leaf_ids, parent_ids, su, rd1, rd2, bp, bm, wl, wu, xv, xe, near):
    return pl.pallas_call(
        field_kernel,
        out_shape=jax.ShapeDtypeStruct((BOXES, 1024), F32),
        in_specs=[SM] * 3 + [VM] * 10,
        out_specs=VM,
        scratch_shapes=[
            pltpu.VMEM((3 * BOXES, 16, 128), BF16),
            pltpu.VMEM((12 * PARENTS, 16, 128), BF16),
            pltpu.VMEM((2, S_ROWS, 128), BF16),
            pltpu.VMEM((BOXES * 16, 128), F32),
            pltpu.VMEM((8 * BOXES, 128), F32),
        ],
        compiler_params=params(),
        name="field",
    )(info, leaf_ids, parent_ids, su, rd1, rd2, bp, bm, wl, wu, xv, xe, near)


def local(
    charges, coords, basis, transfer, leaf_table, upper_table, near_ids, near_count, leaf_ids, parent_ids
):
    flat = ("box", "sub")
    boxes = lax.axis_size("box")
    subs = lax.axis_size("sub")
    chain = boxes * subs
    sub = lax.axis_index("sub")
    info = jnp.stack(
        [
            (lax.axis_index(flat) - 1) * BOXES,
            (lax.axis_index("box") - 1) * PARENTS * subs,
            sub,
        ]
    ).astype(jnp.int32)
    su, xv, xe = run_skeleton(charges, basis, transfer)
    rd1 = lax.ppermute(su, "sub", [(i, i ^ 1) for i in range(subs)])
    own = run_pack(charges, coords)
    before = lax.ppermute(own, flat, [(i, i + 1) for i in range(chain - 1)])
    after = lax.ppermute(own, flat, [(i + 1, i) for i in range(chain - 1)])
    wl, wu = run_tables(leaf_table, upper_table)
    rd2 = lax.ppermute(
        jnp.concatenate([su, rd1[S_ROWS:]], axis=0), "sub", [(i, i ^ 3) for i in range(subs)]
    )
    edge = jnp.concatenate([rd2, su[S_ROWS:], rd1[S_ROWS:]], axis=0)
    bp = lax.ppermute(edge, "box", [(i, i + 1) for i in range(boxes - 1)])
    bm = lax.ppermute(edge, "box", [(i + 1, i) for i in range(boxes - 1)])
    near = run_near(info, near_ids, near_count, own, before, after, coords)
    return run_field(info, leaf_ids, parent_ids, su, rd1, rd2, bp, bm, wl, wu, xv, xe, near)


def solution(mesh):
    rows = P(("box", "sub"), None)
    placed = (rows, rows, rows, rows, P(), P(), rows, P(("box", "sub")), rows, rows)
    return jax.shard_map(
        local, mesh=mesh, in_specs=placed, out_specs=P(("box", "sub"), None), check_vma=False
    )
```

```python
import functools
import math

import jax
import jax.numpy as jnp
from jax import lax
from jax.experimental import pallas as pl
from jax.experimental.pallas import tpu as pltpu
from jax.sharding import PartitionSpec as P

SOFT = 0.05
SCALE = 16.0 * math.pi * math.pi
F32 = jnp.float32
BF16 = jnp.bfloat16
BOXES = 48
PAIRS = BOXES // 2
NEAR = 27
OFFSETS = 96
UPPER = 64
PARENTS = 6
S_ROWS = PAIRS * 16
U_ROWS = PARENTS // 2 * 16
VMEM_LIMIT = 60 * 1024 * 1024


def nn(a, b):
    return lax.dot_general(a, b, (((1,), (0,)), ((), ())), preferred_element_type=F32)


def nt(a, b):
    return lax.dot_general(a, b, (((1,), (1,)), ((), ())), preferred_element_type=F32)


def iota(shape, dim):
    return lax.broadcasted_iota(jnp.int32, shape, dim)


def onehot(cond):
    return jnp.where(cond, 1.0, 0.0).astype(BF16)


def half_swap(x):
    return pltpu.roll(x, 64, 1)


def skeleton_kernel(q_ref, v_ref, e_ref, su_ref, xv_ref, xe_ref, qs, vs, es):
    for i in range(8):
        qs[i * BOXES : (i + 1) * BOXES] = q_ref[:, i * 128 : (i + 1) * 128].astype(F32)
    for t in range(32):
        vs[t * BOXES : (t + 1) * BOXES] = v_ref[:, t * 128 : (t + 1) * 128].astype(F32)
    for t in range(32):
        es[t * BOXES : (t + 1) * BOXES] = e_ref[:, t * 128 : (t + 1) * 128].astype(F32)
    row = iota((32, 128), 0)
    lane = iota((32, 128), 1)
    pick = onehot((lane % 32) == row)
    lane8 = iota((8, 128), 1) // 32
    lane16 = iota((16, 128), 1)
    low = lane16 < 64
    group = lane // 32
    for g in range(BOXES // 4):
        parts = []
        for c in range(4):
            b = g * 4 + c
            rows = qs[pl.ds(b, 8, stride=BOXES), :]
            parts += [jnp.where(lane8 == m, rows, 0.0) for m in range(4)]
        weights = jnp.concatenate(parts, axis=0).astype(BF16)
        q2 = nt(pick, weights)
        lhs = jnp.concatenate([jnp.where(group == c, q2, 0.0) for c in range(4)], axis=0).astype(BF16)
        vb = []
        for c in range(4):
            b = g * 4 + c
            vb += [vs[pl.ds(m * BOXES + b, 8, stride=4 * BOXES), :] for m in range(4)]
        xv = jnp.concatenate(vb, axis=0).astype(BF16)
        xv_ref[g * 128 : (g + 1) * 128] = xv
        z = nn(lhs, xv)
        for u in range(2):
            o = u * 64
            even = z[o : o + 16] + half_swap(z[o + 16 : o + 32])
            odd = half_swap(z[o + 32 : o + 48]) + z[o + 48 : o + 64]
            r = (g * 2 + u) * 16
            su_ref[r : r + 16] = jnp.where(low, even, odd).astype(BF16)
    prow = iota((256, 256), 0)
    pcol = iota((256, 256), 1)
    spread = onehot(
        ((prow // 64) == ((pcol % 128) // 32)) & ((prow % 64) == 2 * (pcol % 32) + pcol // 128)
    )
    lifted = []
    for p in range(PARENTS):
        lhs = []
        xe = []
        for h in range(2):
            g = p * 2 + h
            s = su_ref[g * 32 : g * 32 + 32]
            wide = jnp.concatenate([s[:16], s[16:]], axis=1)
            moved = nn(wide, spread)
            lhs.append(jnp.concatenate([moved[:, :128], moved[:, 128:]], axis=0))
            for c in range(4):
                xe.append(es[pl.ds(g * 4 + c, 32, stride=BOXES), :])
        lhs = jnp.concatenate(lhs, axis=1).astype(BF16)
        xe = jnp.concatenate(xe, axis=0).astype(BF16)
        xe_ref[p * 256 : (p + 1) * 256] = xe
        z = nn(lhs, xe)
        if p % 2 == 0:
            lifted = z[:16] + half_swap(z[16:])
        else:
            other = half_swap(z[:16]) + z[16:]
            r = S_ROWS + (p // 2) * 16
            su_ref[r : r + 16] = jnp.where(low, lifted, other).astype(BF16)


def pack_kernel(q_ref, x_ref, out_ref, qs):
    for i in range(8):
        qs[i * BOXES : (i + 1) * BOXES] = q_ref[:, i * 128 : (i + 1) * 128].astype(F32)
    own = iota((8, 128), 0) == iota((8, 128), 1) // 16
    pick = onehot((iota((16, 128), 1) % 16) == iota((16, 128), 0))
    for u in range(PAIRS):
        parts = []
        for c in range(2):
            rows = qs[pl.ds(u * 2 + c, 8, stride=BOXES), :]
            for i in range(8):
                parts.append(jnp.where(own, jnp.broadcast_to(rows[i : i + 1], (8, 128)), 0.0))
        weights = jnp.concatenate(parts, axis=0).astype(BF16)
        out_ref[u * 16 : u * 16 + 16] = nt(pick, weights).astype(BF16)
    out_ref[S_ROWS : S_ROWS + BOXES] = x_ref[:, :128].astype(BF16)
    out_ref[S_ROWS + BOXES : S_ROWS + 2 * BOXES] = jnp.concatenate(
        [x_ref[:, 128:], jnp.zeros((BOXES, 64), F32)], axis=1
    ).astype(BF16)


def table_kernel(leaf_ref, upper_ref, after_ref, wl_ref, wu_ref, ts):
    low = iota((32, 128), 1) < 64
    for ref, out, count in ((leaf_ref, wl_ref, OFFSETS), (upper_ref, wu_ref, UPPER)):
        for t in range(32):
            ts[t * count : (t + 1) * count] = ref[:, t * 128 : (t + 1) * 128].astype(F32)
        for u in range(count // 2):
            first = ts[pl.ds(2 * u, 32, stride=count), :]
            second = ts[pl.ds(2 * u + 1, 32, stride=count), :]
            even = jnp.where(low, first, half_swap(second))
            odd = jnp.where(low, half_swap(first), second)
            out[:, u * 128 : (u + 1) * 128] = jnp.concatenate([even, odd], axis=0).astype(BF16)


def split3(x):
    a = x.astype(BF16).astype(F32)
    rest = x - a
    b = rest.astype(BF16).astype(F32)
    return a, b, rest - b


def dup_matrix():
    r = iota((128, 256), 0)
    c = iota((128, 256), 1)
    return onehot((r // 64 == c // 128) & (r % 64 == c % 64))


def spread_pairs(src_ref, rows, dst_ref, base):
    wide = nn(src_ref[:rows], dup_matrix()).astype(BF16)
    for u in range(rows // 16):
        dst_ref[base + 2 * u] = wide[u * 16 : u * 16 + 16, :128]
        dst_ref[base + 2 * u + 1] = wide[u * 16 : u * 16 + 16, 128:]


STEP = 8
TOTAL = 3 * BOXES


def near_tables_kernel(own_ref, prev_ref, next_ref, x_ref, after_ref, qt, yt, at, bs):
    for side, ref in enumerate((prev_ref, own_ref, next_ref)):
        spread_pairs(ref, S_ROWS, qt, side * BOXES)
    qt[TOTAL] = jnp.zeros((16, 128), BF16)
    lanes = iota((BOXES, 128), 1) < 64

    def dup3(xy, z):
        flip = half_swap(xy)
        return jnp.where(lanes, xy, flip), jnp.where(lanes, flip, xy), jnp.where(lanes, z, half_swap(z))

    ones = jnp.ones((BOXES, 128), F32)
    zeros = jnp.zeros((BOXES, 128), F32)
    for side, ref in enumerate((prev_ref, own_ref, next_ref)):
        xy = ref[S_ROWS : S_ROWS + BOXES].astype(F32)
        z = ref[S_ROWS + BOXES : S_ROWS + 2 * BOXES].astype(F32)
        y0, y1, y2 = dup3(xy, z)
        n = split3(SCALE * (y0 * y0 + y1 * y1 + y2 * y2))
        for k, v in enumerate((y0, y0, y0, y1, y1, y1, y2, y2, y2, *n, ones, ones, ones, zeros)):
            bs[side, k * BOXES : (k + 1) * BOXES] = v
        for b in range(BOXES):
            yt[side * BOXES + b] = bs[side, pl.ds(b, 16, stride=BOXES), :].astype(BF16)
    yt[TOTAL] = onehot(iota((16, 128), 0) >= 12)
    zx = jnp.concatenate([x_ref[:, 128:], jnp.zeros((BOXES, 64), F32)], axis=1)
    x0, x1, x2 = dup3(x_ref[:, :128], zx)
    n = split3(SCALE * (x0 * x0 + x1 * x1 + x2 * x2 + SOFT))
    cols = []
    for x in (x0, x1, x2):
        cols += list(split3((-2.0 * SCALE) * x))
    for k, v in enumerate((*cols, ones, ones, ones, *n, zeros)):
        bs[3, k * BOXES : (k + 1) * BOXES] = v
    eye = onehot((iota((64, 128), 0) == iota((64, 128), 1)))
    for b in range(BOXES):
        at[b] = nt(eye, bs[3, pl.ds(b, 16, stride=BOXES), :].astype(BF16)).astype(BF16)
    at[BOXES] = jnp.zeros((64, 16), BF16) + onehot(iota((64, 16), 1) == 12)


def near_kernel(info, ids_ref, count_ref, qt, yt, at, after_ref, out_ref, slot_v, slot_s, ks, qs, acc, place, sums, sem):
    first = info[0]
    r48 = iota((BOXES, BOXES), 0)
    counts = jnp.sum(
        jnp.where(r48 == iota((BOXES, BOXES), 1), jnp.broadcast_to(count_ref[...], (BOXES, BOXES)), 0),
        axis=1,
        keepdims=True,
    )
    slot_v[...] = jnp.full((BOXES + 8, 128), TOTAL, jnp.int32)
    slot_v[:BOXES, :NEAR] = jnp.where(iota((BOXES, NEAR), 1) < counts, ids_ref[...] - first, TOTAL)
    slot_v[:BOXES, 32:33] = counts
    slot_v[BOXES : BOXES + 8, 32:33] = jnp.zeros((8, 1), jnp.int32)
    copy = pltpu.make_async_copy(slot_v, slot_s, sem)
    copy.start()
    for b in range(BOXES + 1):
        acc[b] = jnp.zeros((16, 64), F32)
    low = iota((16, 128), 1) < 64
    for j in range(STEP):
        place[STEP + j] = BOXES
        ks[1, j] = jnp.zeros((64, 512), BF16)
        qs[1, j] = jnp.zeros((16, 512), BF16)
    copy.wait()

    def finish(last):
        for j in range(STEP):
            here = place[last * STEP + j]
            acc[here] += nt(qs[last, j], ks[last, j])

    def work(state):
        step, box, chunk = state
        slot = step % 2
        finish(1 - slot)
        for j in range(STEP):
            place[slot * STEP + j] = box
            ys = []
            for c in range(4):
                one = slot_s[box, chunk + 2 * c]
                two = slot_s[box, chunk + 2 * c + 1]
                ys.append(jnp.where(low, yt[one], yt[two]))
                qs[slot, j, :, c * 128 : (c + 1) * 128] = jnp.where(low, qt[one], qt[two])
            d = nn(at[box], jnp.concatenate(ys, axis=1))
            ks[slot, j] = lax.rsqrt(d).astype(BF16)
            more = chunk + 8 < slot_s[box, 32]
            box = jnp.where(more, box, jnp.minimum(box + 1, BOXES))
            chunk = jnp.where(more, chunk + 8, 0)
        return step + 1, box, chunk

    step, _, _ = lax.while_loop(lambda s: s[1] < BOXES, work, (0, 0, 0))
    finish(1 - step % 2)
    lane8 = iota((8, 128), 1) // 16
    for g in range(BOXES // 8):
        rows = jnp.concatenate([acc[g * 8 + c] for c in range(8)], axis=0)
        sums[g] = rows.T
        tiles = [sums[g, pl.ds(s, 8, stride=8), :] for s in range(8)]
        for c in range(8):
            total_tile = None
            for s in range(8):
                moved = tiles[s] if s == c else pltpu.roll(tiles[s], (16 * (s - c)) % 128, 1)
                total_tile = moved if total_tile is None else jnp.where(lane8 == s, moved, total_tile)
            out_ref[pl.ds(g * 8 + c, 8, stride=BOXES), :] = total_tile


def couple(table, w_ref, ids, boxes, offsets, low):
    rows = []
    for b in range(boxes):
        tiles = []
        for o in range(0, offsets, 2):
            one = table[ids[b, o]]
            two = table[ids[b, o + 1]]
            tiles.append(jnp.where(low, one, two))
        rows.append(jnp.concatenate(tiles, axis=1))
    lhs = jnp.concatenate(rows, axis=0)
    return nt(lhs, w_ref[...])


def field_kernel(
    info, leaf_ref, pid_ref, su_ref, rd1_ref, rd2_ref, bp_ref, bm_ref, wl_ref, wu_ref, xv_ref, xe_ref, near_ref,
    out_ref, st, ut, halo, fs, ps, ids_v, ids, pids_v, pids, sems,
):
    first = info[0]
    first_parent = info[1]
    sub = info[2]
    ids_v[:, :OFFSETS] = leaf_ref[...] - first
    pids_v[:PARENTS, :UPPER] = pid_ref[...] - first_parent
    copies = [pltpu.make_async_copy(ids_v, ids, sems.at[0]), pltpu.make_async_copy(pids_v, pids, sems.at[1])]
    for copy in copies:
        copy.start()
    low = iota((16, 128), 1) < 64

    @pl.when(sub == 0)
    def _():
        halo[0] = bp_ref[:S_ROWS]
        halo[1] = rd1_ref[:S_ROWS]

    @pl.when(sub == 1)
    def _():
        halo[0] = rd1_ref[:S_ROWS]
        halo[1] = rd2_ref[:S_ROWS]

    @pl.when(sub == 2)
    def _():
        halo[0] = rd2_ref[:S_ROWS]
        halo[1] = rd1_ref[:S_ROWS]

    @pl.when(sub == 3)
    def _():
        halo[0] = rd1_ref[:S_ROWS]
        halo[1] = bm_ref[:S_ROWS]

    spread_pairs(halo.at[0], S_ROWS, st, 0)
    spread_pairs(su_ref, S_ROWS, st, BOXES)
    spread_pairs(halo.at[1], S_ROWS, st, 2 * BOXES)

    def parents(ref, row, group, flip):
        wide = nn(ref[row : row + U_ROWS], dup_matrix()).astype(BF16)
        at = group * 4 * PARENTS + (sub ^ flip) * PARENTS
        for u in range(PARENTS // 2):
            ut[at + 2 * u] = wide[u * 16 : u * 16 + 16, :128]
            ut[at + 2 * u + 1] = wide[u * 16 : u * 16 + 16, 128:]

    for group, ref in ((0, bp_ref), (2, bm_ref)):
        for j, flip in enumerate((3, 2, 0, 1)):
            parents(ref, S_ROWS + j * U_ROWS, group, flip)
    parents(su_ref, S_ROWS, 1, 0)
    parents(rd1_ref, S_ROWS, 1, 1)
    parents(rd2_ref, S_ROWS, 1, 3)
    parents(rd2_ref, S_ROWS + U_ROWS, 1, 2)

    for copy in copies:
        copy.wait()
    upper = couple(ut, wu_ref, pids, PARENTS, UPPER, low)
    r64 = iota((64, 128), 0)
    c64 = iota((64, 128), 1)
    natural = onehot((c64 % 64) == 2 * (r64 % 32) + r64 // 32)
    upper2 = nn(upper.astype(BF16), natural)
    lane16 = iota((16, 128), 1)
    for p in range(PARENTS):
        u = upper2[p * 16 : p * 16 + 16]
        lhs = jnp.concatenate([jnp.where(low, u, 0.0), jnp.where(low, 0.0, u)], axis=0).astype(BF16)
        down = nt(lhs, xe_ref[p * 256 : (p + 1) * 256])
        for c in range(8):
            tile = down[:, (c // 4) * 128 : (c // 4) * 128 + 128]
            at = (c % 4) * 32
            a = tile[:16] if at == 0 else pltpu.roll(tile[:16], 128 - at, 1)
            b = tile[16:] if at == 32 else pltpu.roll(tile[16:], (160 - at) % 128, 1)
            fs[(p * 8 + c) * 16 : (p * 8 + c + 1) * 16] = jnp.where(lane16 < 32, a, b)
    lane8 = iota((8, 128), 1) // 32
    low64 = iota((16, 128), 1) < 64
    part = couple(st, wl_ref, ids, BOXES, OFFSETS, low)
    field = (part + fs[:, :64]).astype(BF16)
    wide = nn(field, natural)
    for g in range(BOXES // 4):
        parts = []
        for c in range(4):
            f = wide[(g * 4 + c) * 16 : (g * 4 + c + 1) * 16]
            parts += [jnp.where(low64, f, 0.0), jnp.where(low64, 0.0, f)]
        weights = jnp.concatenate(parts, axis=0).astype(BF16)
        far = nt(xv_ref[g * 128 : (g + 1) * 128], weights)
        for c in range(4):
            tile = None
            for m in range(4):
                piece = far[c * 32 + m * 8 : c * 32 + m * 8 + 8]
                if m != c:
                    piece = pltpu.roll(piece, (32 * (m - c)) % 128, 1)
                tile = piece if tile is None else jnp.where(lane8 == m, piece, tile)
            ps[pl.ds(g * 4 + c, 8, stride=BOXES), :] = tile
    for i in range(8):
        rows = slice(i * BOXES, (i + 1) * BOXES)
        out_ref[:, i * 128 : (i + 1) * 128] = near_ref[rows] + ps[rows]


VM = pl.BlockSpec(memory_space=pltpu.VMEM)
SM = pl.BlockSpec(memory_space=pltpu.SMEM)


HB = pl.BlockSpec(memory_space=pl.ANY)
PEAK = 1.0e15


def params():
    return pltpu.CompilerParams(vmem_limit_bytes=VMEM_LIMIT)


def cost(us):
    return pl.CostEstimate(flops=int(us * 1e-6 * PEAK), bytes_accessed=1 << 20, transcendentals=0)


def shape(*dims, dtype=BF16):
    return jax.ShapeDtypeStruct(dims, dtype)


def run_skeleton(charges, basis, transfer):
    return pl.pallas_call(
        skeleton_kernel,
        out_shape=(shape(S_ROWS + U_ROWS, 128), shape(BOXES * 32, 128), shape(BOXES * 32, 128)),
        in_specs=[VM] * 3,
        out_specs=(VM,) * 3,
        scratch_shapes=[
            pltpu.VMEM((8 * BOXES, 128), F32),
            pltpu.VMEM((32 * BOXES, 128), F32),
            pltpu.VMEM((32 * BOXES, 128), F32),
        ],
        compiler_params=params(),
        cost_estimate=cost(4.0),
        name="skeleton",
    )(charges, basis, transfer)


def run_pack(charges, coords):
    return pl.pallas_call(
        pack_kernel,
        out_shape=shape(S_ROWS + 2 * BOXES, 128),
        in_specs=[VM] * 2,
        out_specs=VM,
        scratch_shapes=[pltpu.VMEM((8 * BOXES, 128), F32)],
        compiler_params=params(),
        cost_estimate=cost(2.0),
        name="pack",
    )(charges, coords)


def run_tables(leaf_table, upper_table, su):
    return pl.pallas_call(
        table_kernel,
        out_shape=(shape(64, OFFSETS * 64), shape(64, UPPER * 64)),
        in_specs=[VM] * 2 + [HB],
        out_specs=(VM,) * 2,
        scratch_shapes=[pltpu.VMEM((32 * OFFSETS, 128), F32)],
        compiler_params=params(),
        cost_estimate=cost(4.0),
        name="tables",
    )(leaf_table, upper_table, su)


def run_near_tables(own, before, after, coords, wl):
    return pl.pallas_call(
        near_tables_kernel,
        out_shape=(shape(TOTAL + 1, 16, 128), shape(TOTAL + 1, 16, 128), shape(BOXES + 1, 64, 16)),
        in_specs=[VM] * 4 + [HB],
        out_specs=(VM,) * 3,
        scratch_shapes=[pltpu.VMEM((4, 16 * BOXES, 128), F32)],
        compiler_params=params(),
        cost_estimate=cost(4.0),
        name="near_tables",
    )(own, before, after, coords, wl)


def run_near(info, near_ids, near_count, qt, yt, at, rd2):
    return pl.pallas_call(
        near_kernel,
        out_shape=shape(8 * BOXES, 128, dtype=F32),
        in_specs=[SM] + [VM] * 5 + [HB],
        out_specs=VM,
        scratch_shapes=[
            pltpu.VMEM((BOXES + 8, 128), jnp.int32),
            pltpu.SMEM((BOXES + 8, 128), jnp.int32),
            pltpu.VMEM((2, STEP, 64, 512), BF16),
            pltpu.VMEM((2, STEP, 16, 512), BF16),
            pltpu.VMEM((BOXES + 1, 16, 64), F32),
            pltpu.SMEM((2 * STEP,), jnp.int32),
            pltpu.VMEM((BOXES // 8, 64, 128), F32),
            pltpu.SemaphoreType.DMA,
        ],
        compiler_params=params(),
        cost_estimate=cost(7.0),
        name="near",
    )(info, near_ids, near_count.reshape(1, BOXES), qt, yt, at, rd2)


def run_field(info, leaf_ids, parent_ids, su, rd1, rd2, bp, bm, wl, wu, xv, xe, near):
    return pl.pallas_call(
        field_kernel,
        out_shape=shape(BOXES, 1024, dtype=F32),
        in_specs=[SM] + [VM] * 12,
        out_specs=VM,
        scratch_shapes=[
            pltpu.VMEM((3 * BOXES, 16, 128), BF16),
            pltpu.VMEM((12 * PARENTS, 16, 128), BF16),
            pltpu.VMEM((2, S_ROWS, 128), BF16),
            pltpu.VMEM((BOXES * 16, 128), F32),
            pltpu.VMEM((8 * BOXES, 128), F32),
            pltpu.VMEM((BOXES, 128), jnp.int32),
            pltpu.SMEM((BOXES, 128), jnp.int32),
            pltpu.VMEM((8, 128), jnp.int32),
            pltpu.SMEM((8, 128), jnp.int32),
            pltpu.SemaphoreType.DMA((2,)),
        ],
        compiler_params=params(),
        cost_estimate=cost(9.0),
        name="field",
    )(info, leaf_ids, parent_ids, su, rd1, rd2, bp, bm, wl, wu, xv, xe, near)


def local(
    charges, coords, basis, transfer, leaf_table, upper_table, near_ids, near_count, leaf_ids, parent_ids
):
    flat = ("box", "sub")
    boxes = lax.axis_size("box")
    subs = lax.axis_size("sub")
    chain = boxes * subs
    sub = lax.axis_index("sub")
    info = jnp.stack(
        [
            (lax.axis_index(flat) - 1) * BOXES,
            (lax.axis_index("box") - 1) * PARENTS * subs,
            sub,
        ]
    ).astype(jnp.int32)
    own = run_pack(charges, coords)
    before = lax.ppermute(own, flat, [(i, i + 1) for i in range(chain - 1)])
    after = lax.ppermute(own, flat, [(i + 1, i) for i in range(chain - 1)])
    su, xv, xe = run_skeleton(charges, basis, transfer)
    rd1 = lax.ppermute(su, "sub", [(i, i ^ 1) for i in range(subs)])
    wl, wu = run_tables(leaf_table, upper_table, su)
    rd2 = lax.ppermute(
        jnp.concatenate([su, rd1[S_ROWS:]], axis=0), "sub", [(i, i ^ 3) for i in range(subs)]
    )
    qt, yt, at = run_near_tables(own, before, after, coords, wl)
    edge = jnp.concatenate([rd2, su[S_ROWS:], rd1[S_ROWS:]], axis=0)
    bp = lax.ppermute(edge, "box", [(i, i + 1) for i in range(boxes - 1)])
    bm = lax.ppermute(edge, "box", [(i + 1, i) for i in range(boxes - 1)])
    near = run_near(info, near_ids, near_count, qt, yt, at, rd2)
    return run_field(info, leaf_ids, parent_ids, su, rd1, rd2, bp, bm, wl, wu, xv, xe, near)


def solution(mesh):
    rows = P(("box", "sub"), None)
    placed = (rows, rows, rows, rows, P(), P(), rows, P(("box", "sub")), rows, rows)
    return jax.shard_map(
        local, mesh=mesh, in_specs=placed, out_specs=P(("box", "sub"), None), check_vma=False
    )
```

```python
import functools
import math

import jax
import jax.numpy as jnp
from jax import lax
from jax.experimental import pallas as pl
from jax.experimental.pallas import tpu as pltpu
from jax.sharding import PartitionSpec as P

SOFT = 0.05
SCALE = 16.0 * math.pi * math.pi
F32 = jnp.float32
BF16 = jnp.bfloat16
BOXES = 48
PAIRS = BOXES // 2
NEAR = 27
OFFSETS = 96
UPPER = 64
PARENTS = 6
S_ROWS = PAIRS * 16
U_ROWS = PARENTS // 2 * 16
Q_ROW = S_ROWS
XY_ROW = 2 * S_ROWS
Z_ROW = XY_ROW + BOXES
UP_ROW = Z_ROW + BOXES
ALL_ROWS = UP_ROW + U_ROWS
VMEM_LIMIT = 24 * 1024 * 1024


def nn(a, b):
    return lax.dot_general(a, b, (((1,), (0,)), ((), ())), preferred_element_type=F32)


def nt(a, b):
    return lax.dot_general(a, b, (((1,), (1,)), ((), ())), preferred_element_type=F32)


def iota(shape, dim):
    return lax.broadcasted_iota(jnp.int32, shape, dim)


def onehot(cond):
    return jnp.where(cond, 1.0, 0.0).astype(BF16)


def half_swap(x):
    return pltpu.roll(x, 64, 1)


def skeleton_kernel(
    q_hbm, x_hbm, v_hbm, e_hbm, su_ref, up_ref, xv_ref, xe_ref, q_ref, x_ref, v_ref, e_ref, qs, vs, es, sems
):
    loads = [
        pltpu.make_async_copy(q_hbm, q_ref, sems.at[0]),
        pltpu.make_async_copy(v_hbm, v_ref, sems.at[1]),
        pltpu.make_async_copy(x_hbm, x_ref, sems.at[2]),
        pltpu.make_async_copy(e_hbm, e_ref, sems.at[3]),
    ]
    for load in loads:
        load.start()
    loads[0].wait()
    for i in range(8):
        qs[i * BOXES : (i + 1) * BOXES] = q_ref[:, i * 128 : (i + 1) * 128].astype(F32)
    pack_charges(qs, su_ref)
    loads[2].wait()
    su_ref[XY_ROW : XY_ROW + BOXES] = x_ref[:, :128].astype(BF16)
    su_ref[Z_ROW : Z_ROW + BOXES] = jnp.concatenate(
        [x_ref[:, 128:], jnp.zeros((BOXES, 64), F32)], axis=1
    ).astype(BF16)
    loads[1].wait()
    for t in range(32):
        vs[t * BOXES : (t + 1) * BOXES] = v_ref[:, t * 128 : (t + 1) * 128].astype(F32)
    loads[3].wait()
    for t in range(32):
        es[t * BOXES : (t + 1) * BOXES] = e_ref[:, t * 128 : (t + 1) * 128].astype(F32)
    row = iota((32, 128), 0)
    lane = iota((32, 128), 1)
    pick = onehot((lane % 32) == row)
    lane8 = iota((8, 128), 1) // 32
    lane16 = iota((16, 128), 1)
    low = lane16 < 64
    group = lane // 32
    for g in range(BOXES // 4):
        parts = []
        for c in range(4):
            b = g * 4 + c
            rows = qs[pl.ds(b, 8, stride=BOXES), :]
            parts += [jnp.where(lane8 == m, rows, 0.0) for m in range(4)]
        weights = jnp.concatenate(parts, axis=0).astype(BF16)
        q2 = nt(pick, weights)
        lhs = jnp.concatenate([jnp.where(group == c, q2, 0.0) for c in range(4)], axis=0).astype(BF16)
        vb = []
        for c in range(4):
            b = g * 4 + c
            vb += [vs[pl.ds(m * BOXES + b, 8, stride=4 * BOXES), :] for m in range(4)]
        xv = jnp.concatenate(vb, axis=0).astype(BF16)
        xv_ref[g * 128 : (g + 1) * 128] = xv
        z = nn(lhs, xv)
        for u in range(2):
            o = u * 64
            even = z[o : o + 16] + half_swap(z[o + 16 : o + 32])
            odd = half_swap(z[o + 32 : o + 48]) + z[o + 48 : o + 64]
            r = (g * 2 + u) * 16
            su_ref[r : r + 16] = jnp.where(low, even, odd).astype(BF16)
    prow = iota((256, 256), 0)
    pcol = iota((256, 256), 1)
    spread = onehot(
        ((prow // 64) == ((pcol % 128) // 32)) & ((prow % 64) == 2 * (pcol % 32) + pcol // 128)
    )
    lifted = []
    for p in range(PARENTS):
        lhs = []
        xe = []
        for h in range(2):
            g = p * 2 + h
            s = su_ref[g * 32 : g * 32 + 32]
            wide = jnp.concatenate([s[:16], s[16:]], axis=1)
            moved = nn(wide, spread)
            lhs.append(jnp.concatenate([moved[:, :128], moved[:, 128:]], axis=0))
            for c in range(4):
                xe.append(es[pl.ds(g * 4 + c, 32, stride=BOXES), :])
        lhs = jnp.concatenate(lhs, axis=1).astype(BF16)
        xe = jnp.concatenate(xe, axis=0).astype(BF16)
        xe_ref[p * 256 : (p + 1) * 256] = xe
        z = nn(lhs, xe)
        if p % 2 == 0:
            lifted = z[:16] + half_swap(z[16:])
        else:
            other = half_swap(z[:16]) + z[16:]
            r = UP_ROW + (p // 2) * 16
            su_ref[r : r + 16] = jnp.where(low, lifted, other).astype(BF16)
    up_ref[...] = su_ref[UP_ROW:]


def pack_charges(qs, out_ref):
    own = iota((8, 128), 0) == iota((8, 128), 1) // 16
    pick = onehot((iota((16, 128), 1) % 16) == iota((16, 128), 0))
    for u in range(PAIRS):
        parts = []
        for c in range(2):
            rows = qs[pl.ds(u * 2 + c, 8, stride=BOXES), :]
            for i in range(8):
                parts.append(jnp.where(own, jnp.broadcast_to(rows[i : i + 1], (8, 128)), 0.0))
        weights = jnp.concatenate(parts, axis=0).astype(BF16)
        r = Q_ROW + u * 16
        out_ref[r : r + 16] = nt(pick, weights).astype(BF16)


def table_kernel(leaf_ref, upper_ref, after_ref, wl_ref, wu_ref, ts):
    low = iota((32, 128), 1) < 64
    for ref, out, count in ((leaf_ref, wl_ref, OFFSETS), (upper_ref, wu_ref, UPPER)):
        for t in range(32):
            ts[t * count : (t + 1) * count] = ref[:, t * 128 : (t + 1) * 128].astype(F32)
        for u in range(count // 2):
            first = ts[pl.ds(2 * u, 32, stride=count), :]
            second = ts[pl.ds(2 * u + 1, 32, stride=count), :]
            even = jnp.where(low, first, half_swap(second))
            odd = jnp.where(low, half_swap(first), second)
            out[:, u * 128 : (u + 1) * 128] = jnp.concatenate([even, odd], axis=0).astype(BF16)


def split3(x):
    a = x.astype(BF16).astype(F32)
    rest = x - a
    b = rest.astype(BF16).astype(F32)
    return a, b, rest - b


def dup_matrix():
    r = iota((128, 256), 0)
    c = iota((128, 256), 1)
    return onehot((r // 64 == c // 128) & (r % 64 == c % 64))


def spread_pairs(src_ref, row, rows, dst_ref, base):
    wide = nn(src_ref[row : row + rows], dup_matrix()).astype(BF16)
    for u in range(rows // 16):
        dst_ref[base + 2 * u] = wide[u * 16 : u * 16 + 16, :128]
        dst_ref[base + 2 * u + 1] = wide[u * 16 : u * 16 + 16, 128:]


STEP = 8
TOTAL = 3 * BOXES


def leaf_sides(own_ref, ev_ref, od_ref):
    odd = lax.axis_index("sub") % 2
    return ((1, own_ref), (2 - 2 * odd, ev_ref), (2 * odd, od_ref))


def near_tables_kernel(own_ref, ev_ref, od_ref, x_ref, after_ref, qt, yt, at, bs):
    sides = leaf_sides(own_ref, ev_ref, od_ref)
    for side, ref in sides:
        spread_pairs(ref, Q_ROW, S_ROWS, qt, side * BOXES)
    qt[TOTAL] = jnp.zeros((16, 128), BF16)
    lanes = iota((BOXES, 128), 1) < 64

    def dup3(xy, z):
        flip = half_swap(xy)
        return jnp.where(lanes, xy, flip), jnp.where(lanes, flip, xy), jnp.where(lanes, z, half_swap(z))

    ones = jnp.ones((BOXES, 128), F32)
    zeros = jnp.zeros((BOXES, 128), F32)
    for j, (side, ref) in enumerate(sides):
        xy = ref[XY_ROW : XY_ROW + BOXES].astype(F32)
        z = ref[Z_ROW : Z_ROW + BOXES].astype(F32)
        y0, y1, y2 = dup3(xy, z)
        n = split3(SCALE * (y0 * y0 + y1 * y1 + y2 * y2))
        for k, v in enumerate((y0, y0, y0, y1, y1, y1, y2, y2, y2, *n, ones, ones, ones, zeros)):
            bs[j, k * BOXES : (k + 1) * BOXES] = v
        for b in range(BOXES):
            yt[side * BOXES + b] = bs[j, pl.ds(b, 16, stride=BOXES), :].astype(BF16)
    yt[TOTAL] = onehot(iota((16, 128), 0) >= 12)
    zx = jnp.concatenate([x_ref[:, 128:], jnp.zeros((BOXES, 64), F32)], axis=1)
    x0, x1, x2 = dup3(x_ref[:, :128], zx)
    n = split3(SCALE * (x0 * x0 + x1 * x1 + x2 * x2 + SOFT))
    cols = []
    for x in (x0, x1, x2):
        cols += list(split3((-2.0 * SCALE) * x))
    for k, v in enumerate((*cols, ones, ones, ones, *n, zeros)):
        bs[3, k * BOXES : (k + 1) * BOXES] = v
    eye = onehot((iota((64, 128), 0) == iota((64, 128), 1)))
    for b in range(BOXES):
        at[b] = nt(eye, bs[3, pl.ds(b, 16, stride=BOXES), :].astype(BF16)).astype(BF16)
    at[BOXES] = jnp.zeros((64, 16), BF16) + onehot(iota((64, 16), 1) == 12)


def near_kernel(ids_ref, count_ref, qt, yt, at, after_ref, out_ref, slot_v, slot_s, ks, qs, acc, place, sums, sem):
    first = (lax.axis_index(("box", "sub")) - 1) * BOXES
    counts = count_ref[...]
    slot_v[...] = jnp.full((40, 128), TOTAL, jnp.int32)
    slot_v[:NEAR, :BOXES] = jnp.where(iota((NEAR, BOXES), 0) < counts, ids_ref[...] - first, TOTAL)
    slot_v[32:33] = jnp.zeros((1, 128), jnp.int32)
    slot_v[32:33, :BOXES] = counts
    copy = pltpu.make_async_copy(slot_v, slot_s, sem)
    copy.start()
    for b in range(BOXES + 1):
        acc[b] = jnp.zeros((16, 64), F32)
    low = iota((16, 128), 1) < 64
    for j in range(STEP):
        place[STEP + j] = BOXES
        ks[1, j] = jnp.zeros((64, 512), BF16)
        qs[1, j] = jnp.zeros((16, 512), BF16)
    copy.wait()

    def finish(last):
        for j in range(STEP):
            here = place[last * STEP + j]
            acc[here] += nt(qs[last, j], ks[last, j])

    def work(state):
        step, box, chunk = state
        slot = step % 2
        finish(1 - slot)
        for j in range(STEP):
            place[slot * STEP + j] = box
            ys = []
            for c in range(4):
                one = slot_s[chunk + 2 * c, box]
                two = slot_s[chunk + 2 * c + 1, box]
                ys.append(jnp.where(low, yt[one], yt[two]))
                qs[slot, j, :, c * 128 : (c + 1) * 128] = jnp.where(low, qt[one], qt[two])
            d = nn(at[box], jnp.concatenate(ys, axis=1))
            ks[slot, j] = lax.rsqrt(d).astype(BF16)
            more = chunk + 8 < slot_s[32, box]
            box = jnp.where(more, box, jnp.minimum(box + 1, BOXES))
            chunk = jnp.where(more, chunk + 8, 0)
        return step + 1, box, chunk

    step, _, _ = lax.while_loop(lambda s: s[1] < BOXES, work, (0, 0, 0))
    finish(1 - step % 2)
    lane8 = iota((8, 128), 1) // 16
    for g in range(BOXES // 8):
        rows = jnp.concatenate([acc[g * 8 + c] for c in range(8)], axis=0)
        sums[g] = rows.T
        tiles = [sums[g, pl.ds(s, 8, stride=8), :] for s in range(8)]
        for c in range(8):
            total_tile = None
            for s in range(8):
                moved = tiles[s] if s == c else pltpu.roll(tiles[s], (16 * (s - c)) % 128, 1)
                total_tile = moved if total_tile is None else jnp.where(lane8 == s, moved, total_tile)
            out_ref[pl.ds(g * 8 + c, 8, stride=BOXES), :] = total_tile


def couple(table, w_ref, ids, boxes, offsets, low):
    rows = []
    for b in range(boxes):
        tiles = []
        for o in range(0, offsets, 2):
            one = table[ids[b, o]]
            two = table[ids[b, o + 1]]
            tiles.append(jnp.where(low, one, two))
        rows.append(jnp.concatenate(tiles, axis=1))
    lhs = jnp.concatenate(rows, axis=0)
    return nt(lhs, w_ref[...])


def field_kernel(
    leaf_ref, pid_ref, su_ref, ev_ref, od_ref, x3_ref, be_ref, bo_ref, wl_ref, wu_ref, xv_ref, xe_ref, near_ref,
    out_ref, st, ut, fs, ps, ids_v, ids, pids_v, pids, sems,
):
    first = (lax.axis_index(("box", "sub")) - 1) * BOXES
    first_parent = (lax.axis_index("box") - 1) * 4 * PARENTS
    sub = lax.axis_index("sub")
    ids_v[:, :OFFSETS] = leaf_ref[...] - first
    pids_v[:PARENTS, :UPPER] = pid_ref[...] - first_parent
    copies = [pltpu.make_async_copy(ids_v, ids, sems.at[0]), pltpu.make_async_copy(pids_v, pids, sems.at[1])]
    for copy in copies:
        copy.start()
    low = iota((16, 128), 1) < 64

    for side, ref in leaf_sides(su_ref, ev_ref, od_ref):
        spread_pairs(ref, 0, S_ROWS, st, side * BOXES)
    odd = lax.axis_index("box") % 2

    def parents(ref, row, group, flip):
        spread_pairs(ref, row, U_ROWS, ut, (group * 4 + (sub ^ flip)) * PARENTS)

    for group, ref in ((2 - 2 * odd, be_ref), (2 * odd, bo_ref)):
        for j, flip in enumerate((0, 1, 3, 2)):
            parents(ref, j * U_ROWS, group, flip)
    parents(su_ref, UP_ROW, 1, 0)
    parents(ev_ref, UP_ROW, 1, 1)
    parents(x3_ref, 0, 1, 3)
    parents(x3_ref, U_ROWS, 1, 2)
    for copy in copies:
        copy.wait()
    upper = couple(ut, wu_ref, pids, PARENTS, UPPER, low)
    r64 = iota((64, 128), 0)
    c64 = iota((64, 128), 1)
    natural = onehot((c64 % 64) == 2 * (r64 % 32) + r64 // 32)
    upper2 = nn(upper.astype(BF16), natural)
    lane16 = iota((16, 128), 1)
    for p in range(PARENTS):
        u = upper2[p * 16 : p * 16 + 16]
        lhs = jnp.concatenate([jnp.where(low, u, 0.0), jnp.where(low, 0.0, u)], axis=0).astype(BF16)
        down = nt(lhs, xe_ref[p * 256 : (p + 1) * 256])
        for c in range(8):
            tile = down[:, (c // 4) * 128 : (c // 4) * 128 + 128]
            at = (c % 4) * 32
            a = tile[:16] if at == 0 else pltpu.roll(tile[:16], 128 - at, 1)
            b = tile[16:] if at == 32 else pltpu.roll(tile[16:], (160 - at) % 128, 1)
            fs[(p * 8 + c) * 16 : (p * 8 + c + 1) * 16] = jnp.where(lane16 < 32, a, b)
    lane8 = iota((8, 128), 1) // 32
    low64 = iota((16, 128), 1) < 64
    part = couple(st, wl_ref, ids, BOXES, OFFSETS, low)
    field = (part + fs[:, :64]).astype(BF16)
    wide = nn(field, natural)
    for g in range(BOXES // 4):
        parts = []
        for c in range(4):
            f = wide[(g * 4 + c) * 16 : (g * 4 + c + 1) * 16]
            parts += [jnp.where(low64, f, 0.0), jnp.where(low64, 0.0, f)]
        weights = jnp.concatenate(parts, axis=0).astype(BF16)
        far = nt(xv_ref[g * 128 : (g + 1) * 128], weights)
        for c in range(4):
            tile = None
            for m in range(4):
                piece = far[c * 32 + m * 8 : c * 32 + m * 8 + 8]
                if m != c:
                    piece = pltpu.roll(piece, (32 * (m - c)) % 128, 1)
                tile = piece if tile is None else jnp.where(lane8 == m, piece, tile)
            ps[pl.ds(g * 4 + c, 8, stride=BOXES), :] = tile
    for i in range(8):
        rows = slice(i * BOXES, (i + 1) * BOXES)
        out_ref[:, i * 128 : (i + 1) * 128] = near_ref[rows] + ps[rows]


VM = pl.BlockSpec(memory_space=pltpu.VMEM)
SM = pl.BlockSpec(memory_space=pltpu.SMEM)


HB = pl.BlockSpec(memory_space=pl.ANY)
PEAK = 1.0e15


def params(limit=VMEM_LIMIT):
    return pltpu.CompilerParams(vmem_limit_bytes=limit)


def cost(us):
    return pl.CostEstimate(flops=int(us * 1e-6 * PEAK), bytes_accessed=1 << 20, transcendentals=0)


def shape(*dims, dtype=BF16):
    return jax.ShapeDtypeStruct(dims, dtype)


def run_skeleton(charges, coords, basis, transfer):
    return pl.pallas_call(
        skeleton_kernel,
        out_shape=(shape(ALL_ROWS, 128), shape(U_ROWS, 128), shape(BOXES * 32, 128), shape(BOXES * 32, 128)),
        in_specs=[pl.BlockSpec(memory_space=pltpu.HBM)] * 4,
        out_specs=(VM,) * 4,
        scratch_shapes=[
            pltpu.VMEM((BOXES, 1024), BF16),
            pltpu.VMEM((BOXES, 192), F32),
            pltpu.VMEM((BOXES, 4096), BF16),
            pltpu.VMEM((BOXES, 4096), BF16),
            pltpu.VMEM((8 * BOXES, 128), F32),
            pltpu.VMEM((32 * BOXES, 128), F32),
            pltpu.VMEM((32 * BOXES, 128), F32),
            pltpu.SemaphoreType.DMA((4,)),
        ],
        compiler_params=params(60 << 20),
        cost_estimate=cost(4.0),
        name="skeleton",
    )(charges, coords, basis, transfer)


def run_tables(leaf_table, upper_table, su):
    return pl.pallas_call(
        table_kernel,
        out_shape=(shape(64, OFFSETS * 64), shape(64, UPPER * 64)),
        in_specs=[VM] * 2 + [HB],
        out_specs=(VM,) * 2,
        scratch_shapes=[pltpu.VMEM((32 * OFFSETS, 128), F32)],
        compiler_params=params(),
        cost_estimate=cost(2.0),
        name="tables",
    )(leaf_table, upper_table, su)


def run_near_tables(su, ev, od, coords, wl):
    return pl.pallas_call(
        near_tables_kernel,
        out_shape=(shape(TOTAL + 1, 16, 128), shape(TOTAL + 1, 16, 128), shape(BOXES + 1, 64, 16)),
        in_specs=[VM] * 4 + [HB],
        out_specs=(VM,) * 3,
        scratch_shapes=[pltpu.VMEM((4, 16 * BOXES, 128), F32)],
        compiler_params=params(),
        cost_estimate=cost(1.0),
        name="near_tables",
    )(su, ev, od, coords, wl)


def run_near(near_ids, near_count, qt, yt, at, x3):
    return pl.pallas_call(
        near_kernel,
        out_shape=shape(8 * BOXES, 128, dtype=F32),
        in_specs=[VM] * 5 + [HB],
        out_specs=VM,
        scratch_shapes=[
            pltpu.VMEM((40, 128), jnp.int32),
            pltpu.SMEM((40, 128), jnp.int32),
            pltpu.VMEM((2, STEP, 64, 512), BF16),
            pltpu.VMEM((2, STEP, 16, 512), BF16),
            pltpu.VMEM((BOXES + 1, 16, 64), F32),
            pltpu.SMEM((2 * STEP,), jnp.int32),
            pltpu.VMEM((BOXES // 8, 64, 128), F32),
            pltpu.SemaphoreType.DMA,
        ],
        compiler_params=params(),
        cost_estimate=cost(7.0),
        name="near",
    )(near_ids.T, near_count.reshape(1, BOXES), qt, yt, at, x3)


def run_field(leaf_ids, parent_ids, su, ev, od, x3, be, bo, wl, wu, xv, xe, near):
    return pl.pallas_call(
        field_kernel,
        out_shape=shape(BOXES, 1024, dtype=F32),
        in_specs=[VM] * 13,
        out_specs=VM,
        scratch_shapes=[
            pltpu.VMEM((3 * BOXES, 16, 128), BF16),
            pltpu.VMEM((12 * PARENTS, 16, 128), BF16),
            pltpu.VMEM((BOXES * 16, 128), F32),
            pltpu.VMEM((8 * BOXES, 128), F32),
            pltpu.VMEM((BOXES, 128), jnp.int32),
            pltpu.SMEM((BOXES, 128), jnp.int32),
            pltpu.VMEM((8, 128), jnp.int32),
            pltpu.SMEM((8, 128), jnp.int32),
            pltpu.SemaphoreType.DMA((2,)),
        ],
        compiler_params=params(),
        cost_estimate=cost(9.0),
        name="field",
    )(leaf_ids, parent_ids, su, ev, od, x3, be, bo, wl, wu, xv, xe, near)


def local(
    charges, coords, basis, transfer, leaf_table, upper_table, near_ids, near_count, leaf_ids, parent_ids
):
    flat = ("box", "sub")
    boxes = lax.axis_size("box")
    subs = lax.axis_size("sub")
    chain = boxes * subs
    su, up, xv, xe = run_skeleton(charges, coords, basis, transfer)
    ev = lax.ppermute(su, "sub", [(i, i ^ 1) for i in range(subs)])
    od = lax.ppermute(su, flat, [(i, ((i + 1) ^ 1) - 1) for i in range(1, chain - 1)])
    wl, wu = run_tables(leaf_table, upper_table, su)
    pair = jnp.concatenate([up, ev[UP_ROW:]], axis=0)
    x3 = lax.ppermute(pair, "sub", [(i, i ^ 3) for i in range(subs)])
    qt, yt, at = run_near_tables(su, ev, od, coords, wl)
    branch = jnp.concatenate([pair, x3], axis=0)
    be = lax.ppermute(branch, "box", [(i, i ^ 1) for i in range(boxes)])
    bo = lax.ppermute(branch, "box", [(i, ((i + 1) ^ 1) - 1) for i in range(1, boxes - 1)])
    near = run_near(near_ids, near_count, qt, yt, at, x3)
    return run_field(leaf_ids, parent_ids, su, ev, od, x3, be, bo, wl, wu, xv, xe, near)


def solution(mesh):
    rows = P(("box", "sub"), None)
    placed = (rows, rows, rows, rows, P(), P(), rows, P(("box", "sub")), rows, rows)
    return jax.shard_map(
        local, mesh=mesh, in_specs=placed, out_specs=P(("box", "sub"), None), check_vma=False
    )
```

```python
import functools
import math

import jax
import jax.numpy as jnp
from jax import lax
from jax.experimental import pallas as pl
from jax.experimental.pallas import tpu as pltpu
from jax.sharding import PartitionSpec as P

SOFT = 0.05
SCALE = 16.0 * math.pi * math.pi
F32 = jnp.float32
BF16 = jnp.bfloat16
BOXES = 48
VP = 52
PAIRS = BOXES // 2
NEAR = 27
OFFSETS = 96
UPPER = 64
PARENTS = 6
S_ROWS = PAIRS * 16
U_ROWS = PARENTS // 2 * 16
TOTAL = 3 * BOXES
Q_ROW = S_ROWS
XY_ROW = 2 * S_ROWS
Z_ROW = XY_ROW + BOXES
UP_ROW = Z_ROW + BOXES
ALL_ROWS = UP_ROW + U_ROWS
VMEM_LIMIT = 24 * 1024 * 1024


def nn(a, b):
    return lax.dot_general(a, b, (((1,), (0,)), ((), ())), preferred_element_type=F32)


def nt(a, b):
    return lax.dot_general(a, b, (((1,), (1,)), ((), ())), preferred_element_type=F32)


def iota(shape, dim):
    return lax.broadcasted_iota(jnp.int32, shape, dim)


def onehot(cond):
    return jnp.where(cond, 1.0, 0.0).astype(BF16)


def half_swap(x):
    return pltpu.roll(x, 64, 1)


IN_SHAPES = (
    ((BOXES, 1024), BF16),
    ((BOXES, 192), F32),
    ((NEAR, BOXES), jnp.int32),
    ((1, BOXES), jnp.int32),
    ((BOXES, OFFSETS), jnp.int32),
    ((PARENTS, UPPER), jnp.int32),
    ((BOXES, 4096), BF16),
    ((BOXES, 4096), BF16),
)
SLOT_ROWS = 40
LEAF_ROW = SLOT_ROWS
PID_ROW = LEAF_ROW + BOXES
INT_ROWS = PID_ROW + 8
OUT_SHAPES = (
    ((INT_ROWS, 128), jnp.int32),
    ((BOXES * 32, 128), BF16),
    ((2 * S_ROWS + 2 * BOXES + U_ROWS, 128), BF16),
    ((U_ROWS, 128), BF16),
    ((BOXES * 32, 128), BF16),
)


def prepare_kernel(*refs):
    n, m = len(IN_SHAPES), len(OUT_SHAPES)
    sources, targets = refs[:n], refs[n : n + m]
    ins, outs = refs[n + m : 2 * n + m], refs[2 * n + m : 2 * n + 2 * m]
    qs, vs, es, in_sems, out_sems = refs[2 * n + 2 * m :]
    loads = [pltpu.make_async_copy(sources[j], ins[j], in_sems.at[j]) for j in range(n)]
    stores = [pltpu.make_async_copy(outs[j], targets[j], out_sems.at[j]) for j in range(m)]
    q_ref, x_ref, near_ref, count_ref, leaf_ref, pid_ref, v_ref, e_ref = ins
    int_ref, xv_ref, su_ref, up_ref, xe_ref = outs
    for load in loads:
        load.start()
    loads[0].wait()
    for i in range(8):
        qs[i * VP : i * VP + BOXES] = q_ref[:, i * 128 : (i + 1) * 128].astype(F32)
    pack_charges(qs, su_ref)
    loads[1].wait()
    su_ref[XY_ROW : XY_ROW + BOXES] = x_ref[:, :128].astype(BF16)
    su_ref[Z_ROW : Z_ROW + BOXES] = jnp.concatenate(
        [x_ref[:, 128:], jnp.zeros((BOXES, 64), F32)], axis=1
    ).astype(BF16)
    for j in range(2, 6):
        loads[j].wait()
    first = (lax.axis_index(("box", "sub")) - 1) * BOXES
    counts = count_ref[...]
    int_ref[...] = jnp.full((INT_ROWS, 128), TOTAL, jnp.int32)
    int_ref[:NEAR, :BOXES] = jnp.where(iota((NEAR, BOXES), 0) < counts, near_ref[...] - first, TOTAL)
    int_ref[32:33] = jnp.zeros((1, 128), jnp.int32)
    int_ref[32:33, :BOXES] = counts
    int_ref[LEAF_ROW : LEAF_ROW + BOXES, :OFFSETS] = leaf_ref[...] - first
    int_ref[PID_ROW : PID_ROW + PARENTS, :UPPER] = pid_ref[...] - (lax.axis_index("box") - 1) * 4 * PARENTS
    stores[0].start()
    loads[6].wait()
    for t in range(32):
        vs[t * VP : t * VP + BOXES] = v_ref[:, t * 128 : (t + 1) * 128].astype(F32)
    make_skeletons(qs, vs, xv_ref, su_ref)
    stores[1].start()
    loads[7].wait()
    for t in range(32):
        es[t * VP : t * VP + BOXES] = e_ref[:, t * 128 : (t + 1) * 128].astype(F32)
    make_parents(es, xe_ref, su_ref)
    up_ref[...] = su_ref[UP_ROW:]
    for j in range(2, 5):
        stores[j].start()
    for store in stores:
        store.wait()


def make_skeletons(qs, vs, xv_ref, su_ref):
    row = iota((32, 128), 0)
    lane = iota((32, 128), 1)
    pick = onehot((lane % 32) == row)
    lane8 = iota((8, 128), 1) // 32
    lane16 = iota((16, 128), 1)
    low = lane16 < 64
    group = lane // 32
    for g in range(BOXES // 4):
        parts = []
        for c in range(4):
            b = g * 4 + c
            rows = qs[pl.ds(b, 8, stride=VP), :]
            parts += [jnp.where(lane8 == m, rows, 0.0) for m in range(4)]
        weights = jnp.concatenate(parts, axis=0).astype(BF16)
        q2 = nt(pick, weights)
        lhs = jnp.concatenate([jnp.where(group == c, q2, 0.0) for c in range(4)], axis=0).astype(BF16)
        vb = []
        for c in range(4):
            b = g * 4 + c
            vb += [vs[pl.ds(m * VP + b, 8, stride=4 * VP), :] for m in range(4)]
        xv = jnp.concatenate(vb, axis=0).astype(BF16)
        xv_ref[g * 128 : (g + 1) * 128] = xv
        z = nn(lhs, xv)
        for u in range(2):
            o = u * 64
            even = z[o : o + 16] + half_swap(z[o + 16 : o + 32])
            odd = half_swap(z[o + 32 : o + 48]) + z[o + 48 : o + 64]
            r = (g * 2 + u) * 16
            su_ref[r : r + 16] = jnp.where(low, even, odd).astype(BF16)


def make_parents(es, xe_ref, su_ref):
    low = iota((16, 128), 1) < 64
    prow = iota((256, 256), 0)
    pcol = iota((256, 256), 1)
    spread = onehot(
        ((prow // 64) == ((pcol % 128) // 32)) & ((prow % 64) == 2 * (pcol % 32) + pcol // 128)
    )
    lifted = []
    for p in range(PARENTS):
        lhs = []
        xe = []
        for h in range(2):
            g = p * 2 + h
            s = su_ref[g * 32 : g * 32 + 32]
            wide = jnp.concatenate([s[:16], s[16:]], axis=1)
            moved = nn(wide, spread)
            lhs.append(jnp.concatenate([moved[:, :128], moved[:, 128:]], axis=0))
            for c in range(4):
                xe.append(es[pl.ds(g * 4 + c, 32, stride=VP), :])
        lhs = jnp.concatenate(lhs, axis=1).astype(BF16)
        xe = jnp.concatenate(xe, axis=0).astype(BF16)
        xe_ref[p * 256 : (p + 1) * 256] = xe
        z = nn(lhs, xe)
        if p % 2 == 0:
            lifted = z[:16] + half_swap(z[16:])
        else:
            other = half_swap(z[:16]) + z[16:]
            r = UP_ROW + (p // 2) * 16
            su_ref[r : r + 16] = jnp.where(low, lifted, other).astype(BF16)


def pack_charges(qs, out_ref):
    own = iota((8, 128), 0) == iota((8, 128), 1) // 16
    pick = onehot((iota((16, 128), 1) % 16) == iota((16, 128), 0))
    for u in range(PAIRS):
        parts = []
        for c in range(2):
            rows = qs[pl.ds(u * 2 + c, 8, stride=VP), :]
            for i in range(8):
                parts.append(jnp.where(own, jnp.broadcast_to(rows[i : i + 1], (8, 128)), 0.0))
        weights = jnp.concatenate(parts, axis=0).astype(BF16)
        r = Q_ROW + u * 16
        out_ref[r : r + 16] = nt(pick, weights).astype(BF16)


def turn_table(ref, out, ts, count):
    low = iota((32, 128), 1) < 64
    pitch = count + 4
    for t in range(32):
        ts[t * pitch : t * pitch + count] = ref[:, t * 128 : (t + 1) * 128].astype(F32)
    for u in range(count // 2):
        first = ts[pl.ds(2 * u, 32, stride=pitch), :]
        second = ts[pl.ds(2 * u + 1, 32, stride=pitch), :]
        even = jnp.where(low, first, half_swap(second))
        odd = jnp.where(low, half_swap(first), second)
        out[:, u * 128 : (u + 1) * 128] = jnp.concatenate([even, odd], axis=0).astype(BF16)


def table_kernel(leaf_ref, upper_ref, after_ref, wl_ref, wu_ref, tl, tu):
    turn_table(leaf_ref, wl_ref, tl, OFFSETS)
    turn_table(upper_ref, wu_ref, tu, UPPER)


def split3(x):
    a = x.astype(BF16).astype(F32)
    rest = x - a
    b = rest.astype(BF16).astype(F32)
    return a, b, rest - b


def dup_matrix():
    r = iota((128, 256), 0)
    c = iota((128, 256), 1)
    return onehot((r // 64 == c // 128) & (r % 64 == c % 64))


def spread_pairs(src_ref, row, rows, dst_ref, base):
    wide = nn(src_ref[row : row + rows], dup_matrix()).astype(BF16)
    for u in range(rows // 16):
        dst_ref[base + 2 * u] = wide[u * 16 : u * 16 + 16, :128]
        dst_ref[base + 2 * u + 1] = wide[u * 16 : u * 16 + 16, 128:]


STEP = 8


def leaf_sides(own_ref, ev_ref, od_ref):
    odd = lax.axis_index("sub") % 2
    return ((1, own_ref), (2 - 2 * odd, ev_ref), (2 * odd, od_ref))


def near_tables_kernel(own_ref, ev_ref, od_ref, x_ref, qt, yt, at, bs):
    sides = leaf_sides(own_ref, ev_ref, od_ref)
    for side, ref in sides:
        spread_pairs(ref, Q_ROW, S_ROWS, qt, side * BOXES)
    qt[TOTAL] = jnp.zeros((16, 128), BF16)
    lanes = iota((BOXES, 128), 1) < 64

    def dup3(xy, z):
        flip = half_swap(xy)
        return jnp.where(lanes, xy, flip), jnp.where(lanes, flip, xy), jnp.where(lanes, z, half_swap(z))

    ones = jnp.ones((BOXES, 128), F32)
    zeros = jnp.zeros((BOXES, 128), F32)
    for j, (side, ref) in enumerate(sides):
        xy = ref[XY_ROW : XY_ROW + BOXES].astype(F32)
        z = ref[Z_ROW : Z_ROW + BOXES].astype(F32)
        y0, y1, y2 = dup3(xy, z)
        n = split3(SCALE * (y0 * y0 + y1 * y1 + y2 * y2))
        for k, v in enumerate((y0, y0, y0, y1, y1, y1, y2, y2, y2, *n, ones, ones, ones, zeros)):
            bs[j, k * VP : k * VP + BOXES] = v
        for b in range(BOXES):
            yt[side * BOXES + b] = bs[j, pl.ds(b, 16, stride=VP), :].astype(BF16)
    yt[TOTAL] = onehot(iota((16, 128), 0) >= 12)
    zx = jnp.concatenate([x_ref[:, 128:], jnp.zeros((BOXES, 64), F32)], axis=1)
    x0, x1, x2 = dup3(x_ref[:, :128], zx)
    n = split3(SCALE * (x0 * x0 + x1 * x1 + x2 * x2 + SOFT))
    cols = []
    for x in (x0, x1, x2):
        cols += list(split3((-2.0 * SCALE) * x))
    for k, v in enumerate((*cols, ones, ones, ones, *n, zeros)):
        bs[3, k * VP : k * VP + BOXES] = v
    eye = onehot((iota((64, 128), 0) == iota((64, 128), 1)))
    for b in range(BOXES):
        at[b] = nt(eye, bs[3, pl.ds(b, 16, stride=VP), :].astype(BF16)).astype(BF16)
    at[BOXES] = jnp.zeros((64, 16), BF16) + onehot(iota((64, 16), 1) == 12)


def near_kernel(int_ref, qt, yt, at, after_ref, out_ref, slot_s, ks, qs, acc, place, sums, sem):
    copy = pltpu.make_async_copy(int_ref.at[:SLOT_ROWS], slot_s, sem)
    copy.start()
    for b in range(BOXES + 1):
        acc[b] = jnp.zeros((16, 64), F32)
    low = iota((16, 128), 1) < 64
    for j in range(STEP):
        place[STEP + j] = BOXES
        ks[1, j] = jnp.zeros((64, 512), BF16)
        qs[1, j] = jnp.zeros((16, 512), BF16)
    copy.wait()

    def finish(last):
        for j in range(STEP):
            here = place[last * STEP + j]
            acc[here] += nt(qs[last, j], ks[last, j])

    def work(state):
        step, box, chunk = state
        slot = step % 2
        finish(1 - slot)
        for j in range(STEP):
            place[slot * STEP + j] = box
            ys = []
            for c in range(4):
                one = slot_s[chunk + 2 * c, box]
                two = slot_s[chunk + 2 * c + 1, box]
                ys.append(jnp.where(low, yt[one], yt[two]))
                qs[slot, j, :, c * 128 : (c + 1) * 128] = jnp.where(low, qt[one], qt[two])
            d = nn(at[box], jnp.concatenate(ys, axis=1))
            ks[slot, j] = lax.rsqrt(d).astype(BF16)
            more = chunk + 8 < slot_s[32, box]
            box = jnp.where(more, box, jnp.minimum(box + 1, BOXES))
            chunk = jnp.where(more, chunk + 8, 0)
        return step + 1, box, chunk

    step, _, _ = lax.while_loop(lambda s: s[1] < BOXES, work, (0, 0, 0))
    finish(1 - step % 2)
    lane8 = iota((8, 128), 1) // 16
    for g in range(BOXES // 8):
        rows = jnp.concatenate([acc[g * 8 + c] for c in range(8)], axis=0)
        sums[g] = rows.T
        tiles = [sums[g, pl.ds(s, 8, stride=8), :] for s in range(8)]
        for c in range(8):
            total_tile = None
            for s in range(8):
                moved = tiles[s] if s == c else pltpu.roll(tiles[s], (16 * (s - c)) % 128, 1)
                total_tile = moved if total_tile is None else jnp.where(lane8 == s, moved, total_tile)
            out_ref[pl.ds(g * 8 + c, 8, stride=VP), :] = total_tile


def couple(table, w_ref, ids, boxes, offsets, low):
    rows = []
    for b in range(boxes):
        tiles = []
        for o in range(0, offsets, 2):
            one = table[ids[b, o]]
            two = table[ids[b, o + 1]]
            tiles.append(jnp.where(low, one, two))
        rows.append(jnp.concatenate(tiles, axis=1))
    lhs = jnp.concatenate(rows, axis=0)
    return nt(lhs, w_ref[...])


def leaf_kernel(int_ref, su_ref, ev_ref, od_ref, wl_ref, out_ref, st, ids, sem):
    low = iota((16, 128), 1) < 64
    copy = pltpu.make_async_copy(int_ref.at[LEAF_ROW : LEAF_ROW + BOXES], ids, sem)
    copy.start()
    for side, ref in leaf_sides(su_ref, ev_ref, od_ref):
        spread_pairs(ref, 0, S_ROWS, st, side * BOXES)
    copy.wait()
    out_ref[:, :64] = couple(st, wl_ref, ids, BOXES, OFFSETS, low)


def field_kernel(
    int_ref, up_ref, ev_ref, x3_ref, be_ref, bo_ref, wu_ref, xv_ref, xe_ref, part_ref, near_ref,
    out_ref, ut, fs, ps, pids, sem,
):
    sub = lax.axis_index("sub")
    copy = pltpu.make_async_copy(int_ref.at[PID_ROW:INT_ROWS], pids, sem)
    copy.start()
    low = iota((16, 128), 1) < 64
    odd = lax.axis_index("box") % 2

    def parents(ref, row, group, flip):
        spread_pairs(ref, row, U_ROWS, ut, (group * 4 + (sub ^ flip)) * PARENTS)

    for group, ref in ((2 - 2 * odd, be_ref), (2 * odd, bo_ref)):
        for j, flip in enumerate((0, 1, 3, 2)):
            parents(ref, j * U_ROWS, group, flip)
    parents(up_ref, 0, 1, 0)
    parents(ev_ref, UP_ROW, 1, 1)
    parents(x3_ref, 0, 1, 3)
    parents(x3_ref, U_ROWS, 1, 2)
    copy.wait()
    upper = couple(ut, wu_ref, pids, PARENTS, UPPER, low)
    r64 = iota((64, 128), 0)
    c64 = iota((64, 128), 1)
    natural = onehot((c64 % 64) == 2 * (r64 % 32) + r64 // 32)
    upper2 = nn(upper.astype(BF16), natural)
    lane16 = iota((16, 128), 1)
    for p in range(PARENTS):
        u = upper2[p * 16 : p * 16 + 16]
        lhs = jnp.concatenate([jnp.where(low, u, 0.0), jnp.where(low, 0.0, u)], axis=0).astype(BF16)
        down = nt(lhs, xe_ref[p * 256 : (p + 1) * 256])
        for c in range(8):
            tile = down[:, (c // 4) * 128 : (c // 4) * 128 + 128]
            at = (c % 4) * 32
            a = tile[:16] if at == 0 else pltpu.roll(tile[:16], 128 - at, 1)
            b = tile[16:] if at == 32 else pltpu.roll(tile[16:], (160 - at) % 128, 1)
            fs[(p * 8 + c) * 16 : (p * 8 + c + 1) * 16] = jnp.where(lane16 < 32, a, b)
    lane8 = iota((8, 128), 1) // 32
    low64 = iota((16, 128), 1) < 64
    field = (part_ref[:, :64] + fs[:, :64]).astype(BF16)
    wide = nn(field, natural)
    for g in range(BOXES // 4):
        parts = []
        for c in range(4):
            f = wide[(g * 4 + c) * 16 : (g * 4 + c + 1) * 16]
            parts += [jnp.where(low64, f, 0.0), jnp.where(low64, 0.0, f)]
        weights = jnp.concatenate(parts, axis=0).astype(BF16)
        far = nt(xv_ref[g * 128 : (g + 1) * 128], weights)
        for c in range(4):
            tile = None
            for m in range(4):
                piece = far[c * 32 + m * 8 : c * 32 + m * 8 + 8]
                if m != c:
                    piece = pltpu.roll(piece, (32 * (m - c)) % 128, 1)
                tile = piece if tile is None else jnp.where(lane8 == m, piece, tile)
            ps[pl.ds(g * 4 + c, 8, stride=VP), :] = tile
    for i in range(8):
        rows = slice(i * VP, i * VP + BOXES)
        out_ref[:, i * 128 : (i + 1) * 128] = near_ref[rows] + ps[rows]


VM = pl.BlockSpec(memory_space=pltpu.VMEM)
SM = pl.BlockSpec(memory_space=pltpu.SMEM)


HB = pl.BlockSpec(memory_space=pl.ANY)
PEAK = 1.0e15


def params(limit=VMEM_LIMIT):
    return pltpu.CompilerParams(vmem_limit_bytes=limit)


def cost(us):
    return pl.CostEstimate(flops=int(us * 1e-6 * PEAK), bytes_accessed=1 << 20, transcendentals=0)


def shape(*dims, dtype=BF16):
    return jax.ShapeDtypeStruct(dims, dtype)


def run_prepare(charges, coords, near_ids, near_count, leaf_ids, parent_ids, basis, transfer):
    hbm = pl.BlockSpec(memory_space=pltpu.HBM)
    return pl.pallas_call(
        prepare_kernel,
        out_shape=tuple(jax.ShapeDtypeStruct(d, t) for d, t in OUT_SHAPES),
        in_specs=[hbm] * len(IN_SHAPES),
        out_specs=(hbm,) * len(OUT_SHAPES),
        scratch_shapes=[
            *(pltpu.VMEM(d, t) for d, t in IN_SHAPES),
            *(pltpu.VMEM(d, t) for d, t in OUT_SHAPES),
            pltpu.VMEM((8 * VP, 128), F32),
            pltpu.VMEM((32 * VP, 128), F32),
            pltpu.VMEM((32 * VP, 128), F32),
            pltpu.SemaphoreType.DMA((len(IN_SHAPES),)),
            pltpu.SemaphoreType.DMA((len(OUT_SHAPES),)),
        ],
        compiler_params=params(60 << 20),
        cost_estimate=cost(5.0),
        name="prepare",
    )(
        charges, coords, near_ids.T, near_count.reshape(1, BOXES), leaf_ids, parent_ids, basis, transfer
    )


def run_tables(leaf_table, upper_table, up):
    return pl.pallas_call(
        table_kernel,
        out_shape=(shape(64, OFFSETS * 64), shape(64, UPPER * 64)),
        in_specs=[VM] * 2 + [HB],
        out_specs=(VM,) * 2,
        scratch_shapes=[
            pltpu.VMEM((32 * (OFFSETS + 4), 128), F32),
            pltpu.VMEM((32 * (UPPER + 4), 128), F32),
        ],
        compiler_params=params(),
        cost_estimate=cost(1.0),
        name="tables",
    )(leaf_table, upper_table, up)


def run_near_tables(su, ev, od, coords):
    return pl.pallas_call(
        near_tables_kernel,
        out_shape=(shape(TOTAL + 1, 16, 128), shape(TOTAL + 1, 16, 128), shape(BOXES + 1, 64, 16)),
        in_specs=[VM] * 4,
        out_specs=(VM,) * 3,
        scratch_shapes=[pltpu.VMEM((4, 16 * VP, 128), F32)],
        compiler_params=params(),
        cost_estimate=cost(1.0),
        name="near_tables",
    )(su, ev, od, coords)


def run_near(ints, qt, yt, at, x3):
    return pl.pallas_call(
        near_kernel,
        out_shape=shape(8 * VP, 128, dtype=F32),
        in_specs=[VM] * 4 + [HB],
        out_specs=VM,
        scratch_shapes=[
            pltpu.SMEM((SLOT_ROWS, 128), jnp.int32),
            pltpu.VMEM((2, STEP, 64, 512), BF16),
            pltpu.VMEM((2, STEP, 16, 512), BF16),
            pltpu.VMEM((BOXES + 1, 16, 64), F32),
            pltpu.SMEM((2 * STEP,), jnp.int32),
            pltpu.VMEM((BOXES // 8, 64, 128), F32),
            pltpu.SemaphoreType.DMA,
        ],
        compiler_params=params(),
        cost_estimate=cost(7.0),
        name="near",
    )(ints, qt, yt, at, x3)


def run_leaf(ints, su, ev, od, wl):
    return pl.pallas_call(
        leaf_kernel,
        out_shape=shape(BOXES * 16, 128, dtype=F32),
        in_specs=[VM] * 5,
        out_specs=VM,
        scratch_shapes=[
            pltpu.VMEM((3 * BOXES, 16, 128), BF16),
            pltpu.SMEM((BOXES, 128), jnp.int32),
            pltpu.SemaphoreType.DMA,
        ],
        compiler_params=params(),
        cost_estimate=cost(5.0),
        name="leaf",
    )(ints, su, ev, od, wl)


def run_field(ints, up, ev, x3, be, bo, wu, xv, xe, part, near):
    return pl.pallas_call(
        field_kernel,
        out_shape=shape(BOXES, 1024, dtype=F32),
        in_specs=[VM] * 11,
        out_specs=VM,
        scratch_shapes=[
            pltpu.VMEM((12 * PARENTS, 16, 128), BF16),
            pltpu.VMEM((BOXES * 16, 128), F32),
            pltpu.VMEM((8 * VP, 128), F32),
            pltpu.SMEM((8, 128), jnp.int32),
            pltpu.SemaphoreType.DMA,
        ],
        compiler_params=params(),
        cost_estimate=cost(3.0),
        name="field",
    )(ints, up, ev, x3, be, bo, wu, xv, xe, part, near)


def local(
    charges, coords, basis, transfer, leaf_table, upper_table, near_ids, near_count, leaf_ids, parent_ids
):
    flat = ("box", "sub")
    boxes = lax.axis_size("box")
    subs = lax.axis_size("sub")
    chain = boxes * subs
    ints, xv, su, up, xe = run_prepare(
        charges, coords, near_ids, near_count, leaf_ids, parent_ids, basis, transfer
    )
    ev = lax.ppermute(su, "sub", [(i, i ^ 1) for i in range(subs)])
    od = lax.ppermute(su, flat, [(i, ((i + 1) ^ 1) - 1) for i in range(1, chain - 1)])
    wl, wu = run_tables(leaf_table, upper_table, up)
    pair = jnp.concatenate([up, ev[UP_ROW:]], axis=0)
    x3 = lax.ppermute(pair, "sub", [(i, i ^ 3) for i in range(subs)])
    qt, yt, at = run_near_tables(su, ev, od, coords)
    part = run_leaf(ints, su, ev, od, wl)
    branch = jnp.concatenate([pair, x3], axis=0)
    be = lax.ppermute(branch, "box", [(i, i ^ 1) for i in range(boxes)])
    bo = lax.ppermute(branch, "box", [(i, ((i + 1) ^ 1) - 1) for i in range(1, boxes - 1)])
    near = run_near(ints, qt, yt, at, x3)
    return run_field(ints, up, ev, x3, be, bo, wu, xv, xe, part, near)


def solution(mesh):
    rows = P(("box", "sub"), None)
    placed = (rows, rows, rows, rows, P(), P(), rows, P(("box", "sub")), rows, rows)
    return jax.shard_map(
        local, mesh=mesh, in_specs=placed, out_specs=P(("box", "sub"), None), check_vma=False
    )
```

```python
import functools
import math

import jax
import jax.numpy as jnp
from jax import lax
from jax.experimental import pallas as pl
from jax.experimental.pallas import tpu as pltpu
from jax.sharding import PartitionSpec as P

SOFT = 0.05
SCALE = 16.0 * math.pi * math.pi
F32 = jnp.float32
BF16 = jnp.bfloat16
BOXES = 48
VP = 52
PAIRS = BOXES // 2
NEAR = 27
OFFSETS = 96
UPPER = 64
PARENTS = 6
S_ROWS = PAIRS * 16
U_ROWS = PARENTS // 2 * 16
TOTAL = 3 * BOXES
Q_ROW = S_ROWS
XY_ROW = 2 * S_ROWS
Z_ROW = XY_ROW + BOXES
UP_ROW = Z_ROW + BOXES
ALL_ROWS = UP_ROW + U_ROWS
VMEM_LIMIT = 24 * 1024 * 1024


def nn(a, b):
    return lax.dot_general(a, b, (((1,), (0,)), ((), ())), preferred_element_type=F32)


def nt(a, b):
    return lax.dot_general(a, b, (((1,), (1,)), ((), ())), preferred_element_type=F32)


def iota(shape, dim):
    return lax.broadcasted_iota(jnp.int32, shape, dim)


def onehot(cond):
    return jnp.where(cond, 1.0, 0.0).astype(BF16)


def half_swap(x):
    return pltpu.roll(x, 64, 1)


IN_SHAPES = (
    ((BOXES, 1024), BF16),
    ((BOXES, 192), F32),
    ((NEAR, BOXES), jnp.int32),
    ((1, BOXES), jnp.int32),
    ((BOXES, OFFSETS), jnp.int32),
    ((PARENTS, UPPER), jnp.int32),
    ((BOXES, 4096), BF16),
    ((BOXES, 4096), BF16),
)
SLOT_ROWS = 40
LEAF_ROW = SLOT_ROWS
PID_ROW = LEAF_ROW + BOXES
INT_ROWS = PID_ROW + 8
OUT_SHAPES = (
    ((INT_ROWS, 128), jnp.int32),
    ((BOXES * 32, 128), BF16),
    ((2 * S_ROWS + 2 * BOXES + U_ROWS, 128), BF16),
    ((U_ROWS, 128), BF16),
    ((BOXES * 32, 128), BF16),
)


def prepare_kernel(*refs):
    n, m = len(IN_SHAPES), len(OUT_SHAPES)
    sources, targets = refs[:n], refs[n : n + m]
    ins, outs = refs[n + m : 2 * n + m], refs[2 * n + m : 2 * n + 2 * m]
    qs, vs, es, in_sems, out_sems = refs[2 * n + 2 * m :]
    loads = [pltpu.make_async_copy(sources[j], ins[j], in_sems.at[j]) for j in range(n)]
    stores = [pltpu.make_async_copy(outs[j], targets[j], out_sems.at[j]) for j in range(m)]
    q_ref, x_ref, near_ref, count_ref, leaf_ref, pid_ref, v_ref, e_ref = ins
    int_ref, xv_ref, su_ref, up_ref, xe_ref = outs
    for load in loads:
        load.start()
    loads[0].wait()
    for i in range(8):
        qs[i * VP : i * VP + BOXES] = q_ref[:, i * 128 : (i + 1) * 128].astype(F32)
    pack_charges(qs, su_ref)
    loads[1].wait()
    su_ref[XY_ROW : XY_ROW + BOXES] = x_ref[:, :128].astype(BF16)
    su_ref[Z_ROW : Z_ROW + BOXES] = jnp.concatenate(
        [x_ref[:, 128:], jnp.zeros((BOXES, 64), F32)], axis=1
    ).astype(BF16)
    for j in range(2, 6):
        loads[j].wait()
    first = (lax.axis_index(("box", "sub")) - 1) * BOXES
    counts = count_ref[...]
    int_ref[...] = jnp.full((INT_ROWS, 128), TOTAL, jnp.int32)
    int_ref[:NEAR, :BOXES] = jnp.where(iota((NEAR, BOXES), 0) < counts, near_ref[...] - first, TOTAL)
    int_ref[32:33] = jnp.zeros((1, 128), jnp.int32)
    int_ref[32:33, :BOXES] = counts
    int_ref[LEAF_ROW : LEAF_ROW + BOXES, :OFFSETS] = leaf_ref[...] - first
    int_ref[PID_ROW : PID_ROW + PARENTS, :UPPER] = pid_ref[...] - (lax.axis_index("box") - 1) * 4 * PARENTS
    stores[0].start()
    loads[6].wait()
    for t in range(32):
        vs[t * VP : t * VP + BOXES] = v_ref[:, t * 128 : (t + 1) * 128].astype(F32)
    make_skeletons(qs, vs, xv_ref, su_ref)
    stores[1].start()
    loads[7].wait()
    for t in range(32):
        es[t * VP : t * VP + BOXES] = e_ref[:, t * 128 : (t + 1) * 128].astype(F32)
    make_parents(es, xe_ref, su_ref)
    up_ref[...] = su_ref[UP_ROW:]
    for j in range(2, 5):
        stores[j].start()
    for store in stores:
        store.wait()


def make_skeletons(qs, vs, xv_ref, su_ref):
    row = iota((32, 128), 0)
    lane = iota((32, 128), 1)
    pick = onehot((lane % 32) == row)
    lane8 = iota((8, 128), 1) // 32
    lane16 = iota((16, 128), 1)
    low = lane16 < 64
    group = lane // 32
    for g in range(BOXES // 4):
        parts = []
        for c in range(4):
            b = g * 4 + c
            rows = qs[pl.ds(b, 8, stride=VP), :]
            parts += [jnp.where(lane8 == m, rows, 0.0) for m in range(4)]
        weights = jnp.concatenate(parts, axis=0).astype(BF16)
        q2 = nt(pick, weights)
        lhs = jnp.concatenate([jnp.where(group == c, q2, 0.0) for c in range(4)], axis=0).astype(BF16)
        vb = []
        for c in range(4):
            b = g * 4 + c
            vb += [vs[pl.ds(m * VP + b, 8, stride=4 * VP), :] for m in range(4)]
        xv = jnp.concatenate(vb, axis=0).astype(BF16)
        xv_ref[g * 128 : (g + 1) * 128] = xv
        z = nn(lhs, xv)
        for u in range(2):
            o = u * 64
            even = z[o : o + 16] + half_swap(z[o + 16 : o + 32])
            odd = half_swap(z[o + 32 : o + 48]) + z[o + 48 : o + 64]
            r = (g * 2 + u) * 16
            su_ref[r : r + 16] = jnp.where(low, even, odd).astype(BF16)


def make_parents(es, xe_ref, su_ref):
    low = iota((16, 128), 1) < 64
    prow = iota((256, 256), 0)
    pcol = iota((256, 256), 1)
    spread = onehot(
        ((prow // 64) == ((pcol % 128) // 32)) & ((prow % 64) == 2 * (pcol % 32) + pcol // 128)
    )
    lifted = []
    for p in range(PARENTS):
        lhs = []
        xe = []
        for h in range(2):
            g = p * 2 + h
            s = su_ref[g * 32 : g * 32 + 32]
            wide = jnp.concatenate([s[:16], s[16:]], axis=1)
            moved = nn(wide, spread)
            lhs.append(jnp.concatenate([moved[:, :128], moved[:, 128:]], axis=0))
            for c in range(4):
                xe.append(es[pl.ds(g * 4 + c, 32, stride=VP), :])
        lhs = jnp.concatenate(lhs, axis=1).astype(BF16)
        xe = jnp.concatenate(xe, axis=0).astype(BF16)
        xe_ref[p * 256 : (p + 1) * 256] = xe
        z = nn(lhs, xe)
        if p % 2 == 0:
            lifted = z[:16] + half_swap(z[16:])
        else:
            other = half_swap(z[:16]) + z[16:]
            r = UP_ROW + (p // 2) * 16
            su_ref[r : r + 16] = jnp.where(low, lifted, other).astype(BF16)


def pack_charges(qs, out_ref):
    own = iota((8, 128), 0) == iota((8, 128), 1) // 16
    pick = onehot((iota((16, 128), 1) % 16) == iota((16, 128), 0))
    for u in range(PAIRS):
        parts = []
        for c in range(2):
            rows = qs[pl.ds(u * 2 + c, 8, stride=VP), :]
            for i in range(8):
                parts.append(jnp.where(own, jnp.broadcast_to(rows[i : i + 1], (8, 128)), 0.0))
        weights = jnp.concatenate(parts, axis=0).astype(BF16)
        r = Q_ROW + u * 16
        out_ref[r : r + 16] = nt(pick, weights).astype(BF16)


def turn_table(ref, out, ts, count):
    low = iota((32, 128), 1) < 64
    pitch = count + 4
    for t in range(32):
        ts[t * pitch : t * pitch + count] = ref[:, t * 128 : (t + 1) * 128].astype(F32)
    for u in range(count // 2):
        first = ts[pl.ds(2 * u, 32, stride=pitch), :]
        second = ts[pl.ds(2 * u + 1, 32, stride=pitch), :]
        even = jnp.where(low, first, half_swap(second))
        odd = jnp.where(low, half_swap(first), second)
        out[:, u * 128 : (u + 1) * 128] = jnp.concatenate([even, odd], axis=0).astype(BF16)


def table_kernel(leaf_ref, upper_ref, after_ref, wl_ref, wu_ref, tl, tu):
    turn_table(leaf_ref, wl_ref, tl, OFFSETS)
    turn_table(upper_ref, wu_ref, tu, UPPER)


def split3(x):
    a = x.astype(BF16).astype(F32)
    rest = x - a
    b = rest.astype(BF16).astype(F32)
    return a, b, rest - b


def dup_matrix():
    r = iota((128, 256), 0)
    c = iota((128, 256), 1)
    return onehot((r // 64 == c // 128) & (r % 64 == c % 64))


def spread_pairs(src_ref, row, rows, dst_ref, base):
    wide = nn(src_ref[row : row + rows], dup_matrix()).astype(BF16)
    for u in range(rows // 16):
        dst_ref[base + 2 * u, :16] = wide[u * 16 : u * 16 + 16, :128]
        dst_ref[base + 2 * u + 1, :16] = wide[u * 16 : u * 16 + 16, 128:]


STEP = 12


def leaf_sides(own_ref, ev_ref, od_ref):
    odd = lax.axis_index("sub") % 2
    return ((1, own_ref), (2 - 2 * odd, ev_ref), (2 * odd, od_ref))


def near_tables_kernel(own_ref, ev_ref, od_ref, x_ref, tab, at, bs):
    sides = leaf_sides(own_ref, ev_ref, od_ref)
    for side, ref in sides:
        spread_pairs(ref, Q_ROW, S_ROWS, tab, side * BOXES)
    tab[TOTAL, :16] = jnp.zeros((16, 128), BF16)
    lanes = iota((BOXES, 128), 1) < 64

    def dup3(xy, z):
        flip = half_swap(xy)
        return jnp.where(lanes, xy, flip), jnp.where(lanes, flip, xy), jnp.where(lanes, z, half_swap(z))

    ones = jnp.ones((BOXES, 128), F32)
    zeros = jnp.zeros((BOXES, 128), F32)
    for j, (side, ref) in enumerate(sides):
        xy = ref[XY_ROW : XY_ROW + BOXES].astype(F32)
        z = ref[Z_ROW : Z_ROW + BOXES].astype(F32)
        y0, y1, y2 = dup3(xy, z)
        n = split3(SCALE * (y0 * y0 + y1 * y1 + y2 * y2))
        for k, v in enumerate((y0, y0, y0, y1, y1, y1, y2, y2, y2, *n, ones, ones, ones, zeros)):
            bs[j, k * VP : k * VP + BOXES] = v
        for b in range(BOXES):
            tab[side * BOXES + b, 16:] = bs[j, pl.ds(b, 16, stride=VP), :].astype(BF16)
    tab[TOTAL, 16:] = onehot(iota((16, 128), 0) >= 12)
    zx = jnp.concatenate([x_ref[:, 128:], jnp.zeros((BOXES, 64), F32)], axis=1)
    x0, x1, x2 = dup3(x_ref[:, :128], zx)
    n = split3(SCALE * (x0 * x0 + x1 * x1 + x2 * x2 + SOFT))
    cols = []
    for x in (x0, x1, x2):
        cols += list(split3((-2.0 * SCALE) * x))
    for k, v in enumerate((*cols, ones, ones, ones, *n, zeros)):
        bs[3, k * VP : k * VP + BOXES] = v
    eye = onehot((iota((64, 128), 0) == iota((64, 128), 1)))
    for b in range(BOXES):
        at[b] = nt(eye, bs[3, pl.ds(b, 16, stride=VP), :].astype(BF16)).astype(BF16)
    at[BOXES] = jnp.zeros((64, 16), BF16) + onehot(iota((64, 16), 1) == 12)


def near_kernel(int_ref, tab, at, after_ref, out_ref, slot_s, ks, qs, acc, place, sums, sem):
    copy = pltpu.make_async_copy(int_ref.at[:SLOT_ROWS], slot_s, sem)
    copy.start()
    for b in range(BOXES + 1):
        acc[b] = jnp.zeros((16, 64), F32)
    low = iota((16, 128), 1) < 64
    for j in range(STEP):
        place[STEP + j] = BOXES
        ks[1, j] = jnp.zeros((64, 512), BF16)
        qs[1, j] = jnp.zeros((16, 512), BF16)
    copy.wait()

    def finish(last):
        for j in range(STEP):
            here = place[last * STEP + j]
            acc[here] += nt(qs[last, j], ks[last, j])

    def work(state):
        step, box, chunk = state
        slot = step % 2
        finish(1 - slot)
        for j in range(STEP):
            place[slot * STEP + j] = box
            ys = []
            for c in range(4):
                one = slot_s[chunk + 2 * c, box]
                two = slot_s[chunk + 2 * c + 1, box]
                ys.append(jnp.where(low, tab[one, 16:], tab[two, 16:]))
                qs[slot, j, :, c * 128 : (c + 1) * 128] = jnp.where(low, tab[one, :16], tab[two, :16])
            d = nn(at[box], jnp.concatenate(ys, axis=1))
            ks[slot, j] = lax.rsqrt(d).astype(BF16)
            more = chunk + 8 < slot_s[32, box]
            box = jnp.where(more, box, jnp.minimum(box + 1, BOXES))
            chunk = jnp.where(more, chunk + 8, 0)
        return step + 1, box, chunk

    step, _, _ = lax.while_loop(lambda s: s[1] < BOXES, work, (0, 0, 0))
    finish(1 - step % 2)
    lane8 = iota((8, 128), 1) // 16
    for g in range(BOXES // 8):
        rows = jnp.concatenate([acc[g * 8 + c] for c in range(8)], axis=0)
        sums[g] = rows.T
        tiles = [sums[g, pl.ds(s, 8, stride=8), :] for s in range(8)]
        for c in range(8):
            total_tile = None
            for s in range(8):
                moved = tiles[s] if s == c else pltpu.roll(tiles[s], (16 * (s - c)) % 128, 1)
                total_tile = moved if total_tile is None else jnp.where(lane8 == s, moved, total_tile)
            out_ref[pl.ds(g * 8 + c, 8, stride=VP), :] = total_tile


def couple(table, w_ref, ids, boxes, offsets, low):
    rows = []
    for b in range(boxes):
        tiles = []
        for o in range(0, offsets, 2):
            one = table[ids[b, o]]
            two = table[ids[b, o + 1]]
            tiles.append(jnp.where(low, one, two))
        rows.append(jnp.concatenate(tiles, axis=1))
    lhs = jnp.concatenate(rows, axis=0)
    return nt(lhs, w_ref[...])


def leaf_kernel(int_ref, su_ref, ev_ref, od_ref, wl_ref, out_ref, st, ids, sem):
    low = iota((16, 128), 1) < 64
    copy = pltpu.make_async_copy(int_ref.at[LEAF_ROW : LEAF_ROW + BOXES], ids, sem)
    copy.start()
    for side, ref in leaf_sides(su_ref, ev_ref, od_ref):
        spread_pairs(ref, 0, S_ROWS, st, side * BOXES)
    copy.wait()
    out_ref[:, :64] = couple(st, wl_ref, ids, BOXES, OFFSETS, low)


def field_kernel(
    int_ref, up_ref, ev_ref, x3_ref, be_ref, bo_ref, wu_ref, xv_ref, xe_ref, part_ref, near_ref,
    out_ref, ut, fs, ps, pids, sem,
):
    sub = lax.axis_index("sub")
    copy = pltpu.make_async_copy(int_ref.at[PID_ROW:INT_ROWS], pids, sem)
    copy.start()
    low = iota((16, 128), 1) < 64
    odd = lax.axis_index("box") % 2

    def parents(ref, row, group, flip):
        spread_pairs(ref, row, U_ROWS, ut, (group * 4 + (sub ^ flip)) * PARENTS)

    for group, ref in ((2 - 2 * odd, be_ref), (2 * odd, bo_ref)):
        for j, flip in enumerate((0, 1, 3, 2)):
            parents(ref, j * U_ROWS, group, flip)
    parents(up_ref, 0, 1, 0)
    parents(ev_ref, UP_ROW, 1, 1)
    parents(x3_ref, 0, 1, 3)
    parents(x3_ref, U_ROWS, 1, 2)
    copy.wait()
    upper = couple(ut, wu_ref, pids, PARENTS, UPPER, low)
    r64 = iota((64, 128), 0)
    c64 = iota((64, 128), 1)
    natural = onehot((c64 % 64) == 2 * (r64 % 32) + r64 // 32)
    upper2 = nn(upper.astype(BF16), natural)
    lane16 = iota((16, 128), 1)
    for p in range(PARENTS):
        u = upper2[p * 16 : p * 16 + 16]
        lhs = jnp.concatenate([jnp.where(low, u, 0.0), jnp.where(low, 0.0, u)], axis=0).astype(BF16)
        down = nt(lhs, xe_ref[p * 256 : (p + 1) * 256])
        for c in range(8):
            tile = down[:, (c // 4) * 128 : (c // 4) * 128 + 128]
            at = (c % 4) * 32
            a = tile[:16] if at == 0 else pltpu.roll(tile[:16], 128 - at, 1)
            b = tile[16:] if at == 32 else pltpu.roll(tile[16:], (160 - at) % 128, 1)
            fs[(p * 8 + c) * 16 : (p * 8 + c + 1) * 16] = jnp.where(lane16 < 32, a, b)
    lane8 = iota((8, 128), 1) // 32
    low64 = iota((16, 128), 1) < 64
    field = (part_ref[:, :64] + fs[:, :64]).astype(BF16)
    wide = nn(field, natural)
    for g in range(BOXES // 4):
        parts = []
        for c in range(4):
            f = wide[(g * 4 + c) * 16 : (g * 4 + c + 1) * 16]
            parts += [jnp.where(low64, f, 0.0), jnp.where(low64, 0.0, f)]
        weights = jnp.concatenate(parts, axis=0).astype(BF16)
        far = nt(xv_ref[g * 128 : (g + 1) * 128], weights)
        for c in range(4):
            tile = None
            for m in range(4):
                piece = far[c * 32 + m * 8 : c * 32 + m * 8 + 8]
                if m != c:
                    piece = pltpu.roll(piece, (32 * (m - c)) % 128, 1)
                tile = piece if tile is None else jnp.where(lane8 == m, piece, tile)
            ps[pl.ds(g * 4 + c, 8, stride=VP), :] = tile
    for i in range(8):
        rows = slice(i * VP, i * VP + BOXES)
        out_ref[:, i * 128 : (i + 1) * 128] = near_ref[rows] + ps[rows]


VM = pl.BlockSpec(memory_space=pltpu.VMEM)
SM = pl.BlockSpec(memory_space=pltpu.SMEM)


HB = pl.BlockSpec(memory_space=pl.ANY)
PEAK = 1.0e15


def params(limit=VMEM_LIMIT):
    return pltpu.CompilerParams(vmem_limit_bytes=limit)


def cost(us):
    return pl.CostEstimate(flops=int(us * 1e-6 * PEAK), bytes_accessed=1 << 20, transcendentals=0)


def shape(*dims, dtype=BF16):
    return jax.ShapeDtypeStruct(dims, dtype)


def run_prepare(charges, coords, near_ids, near_count, leaf_ids, parent_ids, basis, transfer):
    hbm = pl.BlockSpec(memory_space=pltpu.HBM)
    return pl.pallas_call(
        prepare_kernel,
        out_shape=tuple(jax.ShapeDtypeStruct(d, t) for d, t in OUT_SHAPES),
        in_specs=[hbm] * len(IN_SHAPES),
        out_specs=(hbm,) * len(OUT_SHAPES),
        scratch_shapes=[
            *(pltpu.VMEM(d, t) for d, t in IN_SHAPES),
            *(pltpu.VMEM(d, t) for d, t in OUT_SHAPES),
            pltpu.VMEM((8 * VP, 128), F32),
            pltpu.VMEM((32 * VP, 128), F32),
            pltpu.VMEM((32 * VP, 128), F32),
            pltpu.SemaphoreType.DMA((len(IN_SHAPES),)),
            pltpu.SemaphoreType.DMA((len(OUT_SHAPES),)),
        ],
        compiler_params=params(60 << 20),
        cost_estimate=cost(5.0),
        name="prepare",
    )(
        charges, coords, near_ids.T, near_count.reshape(1, BOXES), leaf_ids, parent_ids, basis, transfer
    )


def run_tables(leaf_table, upper_table, up):
    return pl.pallas_call(
        table_kernel,
        out_shape=(shape(64, OFFSETS * 64), shape(64, UPPER * 64)),
        in_specs=[VM] * 2 + [HB],
        out_specs=(VM,) * 2,
        scratch_shapes=[
            pltpu.VMEM((32 * (OFFSETS + 4), 128), F32),
            pltpu.VMEM((32 * (UPPER + 4), 128), F32),
        ],
        compiler_params=params(),
        cost_estimate=cost(1.0),
        name="tables",
    )(leaf_table, upper_table, up)


def run_near_tables(su, ev, od, coords):
    return pl.pallas_call(
        near_tables_kernel,
        out_shape=(shape(TOTAL + 1, 32, 128), shape(BOXES + 1, 64, 16)),
        in_specs=[VM] * 4,
        out_specs=(VM,) * 2,
        scratch_shapes=[pltpu.VMEM((4, 16 * VP, 128), F32)],
        compiler_params=params(),
        cost_estimate=cost(1.0),
        name="near_tables",
    )(su, ev, od, coords)


def run_near(ints, tab, at, x3):
    return pl.pallas_call(
        near_kernel,
        out_shape=shape(8 * VP, 128, dtype=F32),
        in_specs=[VM] * 3 + [HB],
        out_specs=VM,
        scratch_shapes=[
            pltpu.SMEM((SLOT_ROWS, 128), jnp.int32),
            pltpu.VMEM((2, STEP, 64, 512), BF16),
            pltpu.VMEM((2, STEP, 16, 512), BF16),
            pltpu.VMEM((BOXES + 1, 16, 64), F32),
            pltpu.SMEM((2 * STEP,), jnp.int32),
            pltpu.VMEM((BOXES // 8, 64, 128), F32),
            pltpu.SemaphoreType.DMA,
        ],
        compiler_params=params(),
        cost_estimate=cost(7.0),
        name="near",
    )(ints, tab, at, x3)


def run_leaf(ints, su, ev, od, wl):
    return pl.pallas_call(
        leaf_kernel,
        out_shape=shape(BOXES * 16, 128, dtype=F32),
        in_specs=[VM] * 5,
        out_specs=VM,
        scratch_shapes=[
            pltpu.VMEM((3 * BOXES, 16, 128), BF16),
            pltpu.SMEM((BOXES, 128), jnp.int32),
            pltpu.SemaphoreType.DMA,
        ],
        compiler_params=params(),
        cost_estimate=cost(5.0),
        name="leaf",
    )(ints, su, ev, od, wl)


def run_field(ints, up, ev, x3, be, bo, wu, xv, xe, part, near):
    return pl.pallas_call(
        field_kernel,
        out_shape=shape(BOXES, 1024, dtype=F32),
        in_specs=[VM] * 11,
        out_specs=VM,
        scratch_shapes=[
            pltpu.VMEM((12 * PARENTS, 16, 128), BF16),
            pltpu.VMEM((BOXES * 16, 128), F32),
            pltpu.VMEM((8 * VP, 128), F32),
            pltpu.SMEM((8, 128), jnp.int32),
            pltpu.SemaphoreType.DMA,
        ],
        compiler_params=params(),
        cost_estimate=cost(3.0),
        name="field",
    )(ints, up, ev, x3, be, bo, wu, xv, xe, part, near)


def local(
    charges, coords, basis, transfer, leaf_table, upper_table, near_ids, near_count, leaf_ids, parent_ids
):
    flat = ("box", "sub")
    boxes = lax.axis_size("box")
    subs = lax.axis_size("sub")
    chain = boxes * subs
    ints, xv, su, up, xe = run_prepare(
        charges, coords, near_ids, near_count, leaf_ids, parent_ids, basis, transfer
    )
    ev = lax.ppermute(su, "sub", [(i, i ^ 1) for i in range(subs)])
    od = lax.ppermute(su, flat, [(i, ((i + 1) ^ 1) - 1) for i in range(1, chain - 1)])
    wl, wu = run_tables(leaf_table, upper_table, up)
    pair = jnp.concatenate([up, ev[UP_ROW:]], axis=0)
    x3 = lax.ppermute(pair, "sub", [(i, i ^ 3) for i in range(subs)])
    tab, at = run_near_tables(su, ev, od, coords)
    part = run_leaf(ints, su, ev, od, wl)
    branch = jnp.concatenate([pair, x3], axis=0)
    be = lax.ppermute(branch, "box", [(i, i ^ 1) for i in range(boxes)])
    bo = lax.ppermute(branch, "box", [(i, ((i + 1) ^ 1) - 1) for i in range(1, boxes - 1)])
    near = run_near(ints, tab, at, x3)
    return run_field(ints, up, ev, x3, be, bo, wu, xv, xe, part, near)


def solution(mesh):
    rows = P(("box", "sub"), None)
    placed = (rows, rows, rows, rows, P(), P(), rows, P(("box", "sub")), rows, rows)
    return jax.shard_map(
        local, mesh=mesh, in_specs=placed, out_specs=P(("box", "sub"), None), check_vma=False
    )
```

```python
import functools
import math

import jax
import jax.numpy as jnp
from jax import lax
from jax.experimental import pallas as pl
from jax.experimental.pallas import tpu as pltpu
from jax.sharding import PartitionSpec as P

SOFT = 0.05
SCALE = 16.0 * math.pi * math.pi
F32 = jnp.float32
BF16 = jnp.bfloat16
BOXES = 48
VP = 52
PAIRS = BOXES // 2
NEAR = 27
OFFSETS = 96
UPPER = 64
PARENTS = 6
S_ROWS = PAIRS * 16
U_ROWS = PARENTS // 2 * 16
TOTAL = 3 * BOXES
Q_ROW = S_ROWS
XY_ROW = 2 * S_ROWS
Z_ROW = XY_ROW + BOXES
UP_ROW = Z_ROW + BOXES
ALL_ROWS = UP_ROW + U_ROWS
VMEM_LIMIT = 24 * 1024 * 1024


def nn(a, b):
    return lax.dot_general(a, b, (((1,), (0,)), ((), ())), preferred_element_type=F32)


def nt(a, b):
    return lax.dot_general(a, b, (((1,), (1,)), ((), ())), preferred_element_type=F32)


def iota(shape, dim):
    return lax.broadcasted_iota(jnp.int32, shape, dim)


def onehot(cond):
    return jnp.where(cond, 1.0, 0.0).astype(BF16)


def half_swap(x):
    return pltpu.roll(x, 64, 1)


IN_SHAPES = (
    ((BOXES, 1024), BF16),
    ((BOXES, 192), F32),
    ((NEAR, BOXES), jnp.int32),
    ((1, BOXES), jnp.int32),
    ((BOXES, OFFSETS), jnp.int32),
    ((PARENTS, UPPER), jnp.int32),
    ((BOXES, 4096), BF16),
    ((BOXES, 4096), BF16),
)
SLOT_ROWS = 40
LEAF_ROW = SLOT_ROWS
PID_ROW = LEAF_ROW + BOXES
INT_ROWS = PID_ROW + 8
OUT_SHAPES = (
    ((INT_ROWS, 128), jnp.int32),
    ((BOXES * 32, 128), BF16),
    ((2 * S_ROWS + 2 * BOXES + U_ROWS, 128), BF16),
    ((U_ROWS, 128), BF16),
    ((BOXES * 32, 128), BF16),
)


def prepare_kernel(*refs):
    n, m = len(IN_SHAPES), len(OUT_SHAPES)
    sources, targets = refs[:n], refs[n : n + m]
    ins, outs = refs[n + m : 2 * n + m], refs[2 * n + m : 2 * n + 2 * m]
    qs, vs, es, in_sems, out_sems = refs[2 * n + 2 * m :]
    loads = [pltpu.make_async_copy(sources[j], ins[j], in_sems.at[j]) for j in range(n)]
    stores = [pltpu.make_async_copy(outs[j], targets[j], out_sems.at[j]) for j in range(m)]
    q_ref, x_ref, near_ref, count_ref, leaf_ref, pid_ref, v_ref, e_ref = ins
    int_ref, xv_ref, su_ref, up_ref, xe_ref = outs
    for load in loads:
        load.start()
    loads[0].wait()
    for i in range(8):
        qs[i * VP : i * VP + BOXES] = q_ref[:, i * 128 : (i + 1) * 128].astype(F32)
    pack_charges(qs, su_ref)
    loads[1].wait()
    su_ref[XY_ROW : XY_ROW + BOXES] = x_ref[:, :128].astype(BF16)
    su_ref[Z_ROW : Z_ROW + BOXES] = jnp.concatenate(
        [x_ref[:, 128:], jnp.zeros((BOXES, 64), F32)], axis=1
    ).astype(BF16)
    for j in range(2, 6):
        loads[j].wait()
    first = (lax.axis_index(("box", "sub")) - 1) * BOXES
    counts = count_ref[...]
    int_ref[...] = jnp.full((INT_ROWS, 128), TOTAL, jnp.int32)
    int_ref[:NEAR, :BOXES] = jnp.where(iota((NEAR, BOXES), 0) < counts, near_ref[...] - first, TOTAL)
    int_ref[32:33] = jnp.zeros((1, 128), jnp.int32)
    int_ref[32:33, :BOXES] = counts
    int_ref[LEAF_ROW : LEAF_ROW + BOXES, :OFFSETS] = leaf_ref[...] - first
    int_ref[PID_ROW : PID_ROW + PARENTS, :UPPER] = pid_ref[...] - (lax.axis_index("box") - 1) * 4 * PARENTS
    stores[0].start()
    loads[6].wait()
    for t in range(32):
        vs[t * VP : t * VP + BOXES] = v_ref[:, t * 128 : (t + 1) * 128].astype(F32)
    make_skeletons(qs, vs, xv_ref, su_ref)
    stores[1].start()
    loads[7].wait()
    for t in range(32):
        es[t * VP : t * VP + BOXES] = e_ref[:, t * 128 : (t + 1) * 128].astype(F32)
    make_parents(es, xe_ref, su_ref)
    up_ref[...] = su_ref[UP_ROW:]
    for j in range(2, 5):
        stores[j].start()
    for store in stores:
        store.wait()


def make_skeletons(qs, vs, xv_ref, su_ref):
    row = iota((32, 128), 0)
    lane = iota((32, 128), 1)
    pick = onehot((lane % 32) == row)
    lane8 = iota((8, 128), 1) // 32
    lane16 = iota((16, 128), 1)
    low = lane16 < 64
    group = lane // 32
    for g in range(BOXES // 4):
        parts = []
        for c in range(4):
            b = g * 4 + c
            rows = qs[pl.ds(b, 8, stride=VP), :]
            parts += [jnp.where(lane8 == m, rows, 0.0) for m in range(4)]
        weights = jnp.concatenate(parts, axis=0).astype(BF16)
        q2 = nt(pick, weights)
        lhs = jnp.concatenate([jnp.where(group == c, q2, 0.0) for c in range(4)], axis=0).astype(BF16)
        vb = []
        for c in range(4):
            b = g * 4 + c
            vb += [vs[pl.ds(m * VP + b, 8, stride=4 * VP), :] for m in range(4)]
        xv = jnp.concatenate(vb, axis=0).astype(BF16)
        xv_ref[g * 128 : (g + 1) * 128] = xv
        z = nn(lhs, xv)
        for u in range(2):
            o = u * 64
            even = z[o : o + 16] + half_swap(z[o + 16 : o + 32])
            odd = half_swap(z[o + 32 : o + 48]) + z[o + 48 : o + 64]
            r = (g * 2 + u) * 16
            su_ref[r : r + 16] = jnp.where(low, even, odd).astype(BF16)


def make_parents(es, xe_ref, su_ref):
    low = iota((16, 128), 1) < 64
    prow = iota((256, 256), 0)
    pcol = iota((256, 256), 1)
    spread = onehot(
        ((prow // 64) == ((pcol % 128) // 32)) & ((prow % 64) == 2 * (pcol % 32) + pcol // 128)
    )
    lifted = []
    for p in range(PARENTS):
        lhs = []
        xe = []
        for h in range(2):
            g = p * 2 + h
            s = su_ref[g * 32 : g * 32 + 32]
            wide = jnp.concatenate([s[:16], s[16:]], axis=1)
            moved = nn(wide, spread)
            lhs.append(jnp.concatenate([moved[:, :128], moved[:, 128:]], axis=0))
            for c in range(4):
                xe.append(es[pl.ds(g * 4 + c, 32, stride=VP), :])
        lhs = jnp.concatenate(lhs, axis=1).astype(BF16)
        xe = jnp.concatenate(xe, axis=0).astype(BF16)
        xe_ref[p * 256 : (p + 1) * 256] = xe
        z = nn(lhs, xe)
        if p % 2 == 0:
            lifted = z[:16] + half_swap(z[16:])
        else:
            other = half_swap(z[:16]) + z[16:]
            r = UP_ROW + (p // 2) * 16
            su_ref[r : r + 16] = jnp.where(low, lifted, other).astype(BF16)


def pack_charges(qs, out_ref):
    own = iota((8, 128), 0) == iota((8, 128), 1) // 16
    pick = onehot((iota((16, 128), 1) % 16) == iota((16, 128), 0))
    for u in range(PAIRS):
        parts = []
        for c in range(2):
            rows = qs[pl.ds(u * 2 + c, 8, stride=VP), :]
            for i in range(8):
                parts.append(jnp.where(own, jnp.broadcast_to(rows[i : i + 1], (8, 128)), 0.0))
        weights = jnp.concatenate(parts, axis=0).astype(BF16)
        r = Q_ROW + u * 16
        out_ref[r : r + 16] = nt(pick, weights).astype(BF16)


def turn_table(ref, out, ts, count):
    low = iota((32, 128), 1) < 64
    pitch = count + 4
    for t in range(32):
        ts[t * pitch : t * pitch + count] = ref[:, t * 128 : (t + 1) * 128].astype(F32)
    for u in range(count // 2):
        first = ts[pl.ds(2 * u, 32, stride=pitch), :]
        second = ts[pl.ds(2 * u + 1, 32, stride=pitch), :]
        even = jnp.where(low, first, half_swap(second))
        odd = jnp.where(low, half_swap(first), second)
        out[:, u * 128 : (u + 1) * 128] = jnp.concatenate([even, odd], axis=0).astype(BF16)


def table_kernel(leaf_ref, upper_ref, after_ref, wl_ref, wu_ref, tl, tu):
    turn_table(leaf_ref, wl_ref, tl, OFFSETS)
    turn_table(upper_ref, wu_ref, tu, UPPER)


def split3(x):
    a = x.astype(BF16).astype(F32)
    rest = x - a
    b = rest.astype(BF16).astype(F32)
    return a, b, rest - b


def dup_matrix():
    r = iota((128, 256), 0)
    c = iota((128, 256), 1)
    return onehot((r // 64 == c // 128) & (r % 64 == c % 64))


def spread_pairs(src_ref, row, rows, dst_ref, base):
    wide = nn(src_ref[row : row + rows], dup_matrix()).astype(BF16)
    for u in range(rows // 16):
        dst_ref[base + 2 * u, :16] = wide[u * 16 : u * 16 + 16, :128]
        dst_ref[base + 2 * u + 1, :16] = wide[u * 16 : u * 16 + 16, 128:]


STEP = 16


def leaf_sides(own_ref, ev_ref, od_ref):
    odd = lax.axis_index("sub") % 2
    return ((1, own_ref), (2 - 2 * odd, ev_ref), (2 * odd, od_ref))


def near_tables_kernel(own_ref, ev_ref, od_ref, x_ref, tab, at, bs):
    sides = leaf_sides(own_ref, ev_ref, od_ref)
    for side, ref in sides:
        spread_pairs(ref, Q_ROW, S_ROWS, tab, side * BOXES)
    tab[TOTAL, :16] = jnp.zeros((16, 128), BF16)
    lanes = iota((BOXES, 128), 1) < 64

    def dup3(xy, z):
        flip = half_swap(xy)
        return jnp.where(lanes, xy, flip), jnp.where(lanes, flip, xy), jnp.where(lanes, z, half_swap(z))

    ones = jnp.ones((BOXES, 128), F32)
    zeros = jnp.zeros((BOXES, 128), F32)
    for j, (side, ref) in enumerate(sides):
        xy = ref[XY_ROW : XY_ROW + BOXES].astype(F32)
        z = ref[Z_ROW : Z_ROW + BOXES].astype(F32)
        y0, y1, y2 = dup3(xy, z)
        n = split3(SCALE * (y0 * y0 + y1 * y1 + y2 * y2))
        for k, v in enumerate((y0, y0, y0, y1, y1, y1, y2, y2, y2, *n, ones, ones, ones, zeros)):
            bs[j, k * VP : k * VP + BOXES] = v
        for b in range(BOXES):
            tab[side * BOXES + b, 16:] = bs[j, pl.ds(b, 16, stride=VP), :].astype(BF16)
    tab[TOTAL, 16:] = onehot(iota((16, 128), 0) >= 12)
    zx = jnp.concatenate([x_ref[:, 128:], jnp.zeros((BOXES, 64), F32)], axis=1)
    x0, x1, x2 = dup3(x_ref[:, :128], zx)
    n = split3(SCALE * (x0 * x0 + x1 * x1 + x2 * x2 + SOFT))
    cols = []
    for x in (x0, x1, x2):
        cols += list(split3((-2.0 * SCALE) * x))
    for k, v in enumerate((*cols, ones, ones, ones, *n, zeros)):
        bs[3, k * VP : k * VP + BOXES] = v
    eye = onehot((iota((64, 128), 0) == iota((64, 128), 1)))
    for b in range(BOXES):
        at[b] = nt(eye, bs[3, pl.ds(b, 16, stride=VP), :].astype(BF16)).astype(BF16)
    at[BOXES] = jnp.zeros((64, 16), BF16) + onehot(iota((64, 16), 1) == 12)


def near_kernel(int_ref, tab, at, after_ref, out_ref, slot_s, ks, qs, acc, place, sums, sem):
    copy = pltpu.make_async_copy(int_ref.at[:SLOT_ROWS], slot_s, sem)
    copy.start()
    for b in range(BOXES + 1):
        acc[b] = jnp.zeros((16, 64), F32)
    low = iota((16, 128), 1) < 64
    for j in range(STEP):
        place[STEP + j] = BOXES
        ks[1, j] = jnp.zeros((64, 512), BF16)
        qs[1, j] = jnp.zeros((16, 512), BF16)
    copy.wait()

    def finish(last):
        for j in range(STEP):
            here = place[last * STEP + j]
            acc[here] += nt(qs[last, j], ks[last, j])

    def work(state):
        step, box, chunk = state
        slot = step % 2
        finish(1 - slot)
        for j in range(STEP):
            place[slot * STEP + j] = box
            ys = []
            for c in range(4):
                one = slot_s[chunk + 2 * c, box]
                two = slot_s[chunk + 2 * c + 1, box]
                ys.append(jnp.where(low, tab[one, 16:], tab[two, 16:]))
                qs[slot, j, :, c * 128 : (c + 1) * 128] = jnp.where(low, tab[one, :16], tab[two, :16])
            d = nn(at[box], jnp.concatenate(ys, axis=1))
            ks[slot, j] = lax.rsqrt(d).astype(BF16)
            more = chunk + 8 < slot_s[32, box]
            box = jnp.where(more, box, jnp.minimum(box + 1, BOXES))
            chunk = jnp.where(more, chunk + 8, 0)
        return step + 1, box, chunk

    step, _, _ = lax.while_loop(lambda s: s[1] < BOXES, work, (0, 0, 0))
    finish(1 - step % 2)
    lane8 = iota((8, 128), 1) // 16
    for g in range(BOXES // 8):
        rows = jnp.concatenate([acc[g * 8 + c] for c in range(8)], axis=0)
        sums[g] = rows.T
        tiles = [sums[g, pl.ds(s, 8, stride=8), :] for s in range(8)]
        for c in range(8):
            total_tile = None
            for s in range(8):
                moved = tiles[s] if s == c else pltpu.roll(tiles[s], (16 * (s - c)) % 128, 1)
                total_tile = moved if total_tile is None else jnp.where(lane8 == s, moved, total_tile)
            out_ref[pl.ds(g * 8 + c, 8, stride=VP), :] = total_tile


def couple(table, w_ref, ids, boxes, offsets, low):
    rows = []
    for b in range(boxes):
        tiles = []
        for o in range(0, offsets, 2):
            one = table[ids[b, o]]
            two = table[ids[b, o + 1]]
            tiles.append(jnp.where(low, one, two))
        rows.append(jnp.concatenate(tiles, axis=1))
    lhs = jnp.concatenate(rows, axis=0)
    return nt(lhs, w_ref[...])


def leaf_kernel(int_ref, su_ref, ev_ref, od_ref, wl_ref, out_ref, st, ids, sem):
    low = iota((16, 128), 1) < 64
    copy = pltpu.make_async_copy(int_ref.at[LEAF_ROW : LEAF_ROW + BOXES], ids, sem)
    copy.start()
    for side, ref in leaf_sides(su_ref, ev_ref, od_ref):
        spread_pairs(ref, 0, S_ROWS, st, side * BOXES)
    copy.wait()
    out_ref[:, :64] = couple(st, wl_ref, ids, BOXES, OFFSETS, low)


def field_kernel(
    int_ref, up_ref, ev_ref, x3_ref, be_ref, bo_ref, wu_ref, xv_ref, xe_ref, part_ref, near_ref,
    out_ref, ut, fs, ps, pids, sem,
):
    sub = lax.axis_index("sub")
    copy = pltpu.make_async_copy(int_ref.at[PID_ROW:INT_ROWS], pids, sem)
    copy.start()
    low = iota((16, 128), 1) < 64
    odd = lax.axis_index("box") % 2

    def parents(ref, row, group, flip):
        spread_pairs(ref, row, U_ROWS, ut, (group * 4 + (sub ^ flip)) * PARENTS)

    for group, ref in ((2 - 2 * odd, be_ref), (2 * odd, bo_ref)):
        for j, flip in enumerate((0, 1, 3, 2)):
            parents(ref, j * U_ROWS, group, flip)
    parents(up_ref, 0, 1, 0)
    parents(ev_ref, UP_ROW, 1, 1)
    parents(x3_ref, 0, 1, 3)
    parents(x3_ref, U_ROWS, 1, 2)
    copy.wait()
    upper = couple(ut, wu_ref, pids, PARENTS, UPPER, low)
    r64 = iota((64, 128), 0)
    c64 = iota((64, 128), 1)
    natural = onehot((c64 % 64) == 2 * (r64 % 32) + r64 // 32)
    upper2 = nn(upper.astype(BF16), natural)
    lane16 = iota((16, 128), 1)
    for p in range(PARENTS):
        u = upper2[p * 16 : p * 16 + 16]
        lhs = jnp.concatenate([jnp.where(low, u, 0.0), jnp.where(low, 0.0, u)], axis=0).astype(BF16)
        down = nt(lhs, xe_ref[p * 256 : (p + 1) * 256])
        for c in range(8):
            tile = down[:, (c // 4) * 128 : (c // 4) * 128 + 128]
            at = (c % 4) * 32
            a = tile[:16] if at == 0 else pltpu.roll(tile[:16], 128 - at, 1)
            b = tile[16:] if at == 32 else pltpu.roll(tile[16:], (160 - at) % 128, 1)
            fs[(p * 8 + c) * 16 : (p * 8 + c + 1) * 16] = jnp.where(lane16 < 32, a, b)
    lane8 = iota((8, 128), 1) // 32
    low64 = iota((16, 128), 1) < 64
    field = (part_ref[:, :64] + fs[:, :64]).astype(BF16)
    wide = nn(field, natural)
    for g in range(BOXES // 4):
        parts = []
        for c in range(4):
            f = wide[(g * 4 + c) * 16 : (g * 4 + c + 1) * 16]
            parts += [jnp.where(low64, f, 0.0), jnp.where(low64, 0.0, f)]
        weights = jnp.concatenate(parts, axis=0).astype(BF16)
        far = nt(xv_ref[g * 128 : (g + 1) * 128], weights)
        for c in range(4):
            tile = None
            for m in range(4):
                piece = far[c * 32 + m * 8 : c * 32 + m * 8 + 8]
                if m != c:
                    piece = pltpu.roll(piece, (32 * (m - c)) % 128, 1)
                tile = piece if tile is None else jnp.where(lane8 == m, piece, tile)
            ps[pl.ds(g * 4 + c, 8, stride=VP), :] = tile
    for i in range(8):
        rows = slice(i * VP, i * VP + BOXES)
        out_ref[:, i * 128 : (i + 1) * 128] = near_ref[rows] + ps[rows]


VM = pl.BlockSpec(memory_space=pltpu.VMEM)
SM = pl.BlockSpec(memory_space=pltpu.SMEM)


HB = pl.BlockSpec(memory_space=pl.ANY)
PEAK = 1.0e15


def params(limit=VMEM_LIMIT):
    return pltpu.CompilerParams(vmem_limit_bytes=limit)


def cost(us):
    return pl.CostEstimate(flops=int(us * 1e-6 * PEAK), bytes_accessed=1 << 20, transcendentals=0)


def shape(*dims, dtype=BF16):
    return jax.ShapeDtypeStruct(dims, dtype)


def run_prepare(charges, coords, near_ids, near_count, leaf_ids, parent_ids, basis, transfer):
    hbm = pl.BlockSpec(memory_space=pltpu.HBM)
    return pl.pallas_call(
        prepare_kernel,
        out_shape=tuple(jax.ShapeDtypeStruct(d, t) for d, t in OUT_SHAPES),
        in_specs=[hbm] * len(IN_SHAPES),
        out_specs=(hbm,) * len(OUT_SHAPES),
        scratch_shapes=[
            *(pltpu.VMEM(d, t) for d, t in IN_SHAPES),
            *(pltpu.VMEM(d, t) for d, t in OUT_SHAPES),
            pltpu.VMEM((8 * VP, 128), F32),
            pltpu.VMEM((32 * VP, 128), F32),
            pltpu.VMEM((32 * VP, 128), F32),
            pltpu.SemaphoreType.DMA((len(IN_SHAPES),)),
            pltpu.SemaphoreType.DMA((len(OUT_SHAPES),)),
        ],
        compiler_params=params(60 << 20),
        cost_estimate=cost(5.0),
        name="prepare",
    )(
        charges, coords, near_ids.T, near_count.reshape(1, BOXES), leaf_ids, parent_ids, basis, transfer
    )


def run_tables(leaf_table, upper_table, up):
    return pl.pallas_call(
        table_kernel,
        out_shape=(shape(64, OFFSETS * 64), shape(64, UPPER * 64)),
        in_specs=[VM] * 2 + [HB],
        out_specs=(VM,) * 2,
        scratch_shapes=[
            pltpu.VMEM((32 * (OFFSETS + 4), 128), F32),
            pltpu.VMEM((32 * (UPPER + 4), 128), F32),
        ],
        compiler_params=params(),
        cost_estimate=cost(1.0),
        name="tables",
    )(leaf_table, upper_table, up)


def run_near_tables(su, ev, od, coords):
    return pl.pallas_call(
        near_tables_kernel,
        out_shape=(shape(TOTAL + 1, 32, 128), shape(BOXES + 1, 64, 16)),
        in_specs=[VM] * 4,
        out_specs=(VM,) * 2,
        scratch_shapes=[pltpu.VMEM((4, 16 * VP, 128), F32)],
        compiler_params=params(),
        cost_estimate=cost(1.0),
        name="near_tables",
    )(su, ev, od, coords)


def run_near(ints, tab, at, x3):
    return pl.pallas_call(
        near_kernel,
        out_shape=shape(8 * VP, 128, dtype=F32),
        in_specs=[VM] * 3 + [HB],
        out_specs=VM,
        scratch_shapes=[
            pltpu.SMEM((SLOT_ROWS, 128), jnp.int32),
            pltpu.VMEM((2, STEP, 64, 512), BF16),
            pltpu.VMEM((2, STEP, 16, 512), BF16),
            pltpu.VMEM((BOXES + 1, 16, 64), F32),
            pltpu.SMEM((2 * STEP,), jnp.int32),
            pltpu.VMEM((BOXES // 8, 64, 128), F32),
            pltpu.SemaphoreType.DMA,
        ],
        compiler_params=params(),
        cost_estimate=cost(7.0),
        name="near",
    )(ints, tab, at, x3)


def run_leaf(ints, su, ev, od, wl):
    return pl.pallas_call(
        leaf_kernel,
        out_shape=shape(BOXES * 16, 128, dtype=F32),
        in_specs=[VM] * 5,
        out_specs=VM,
        scratch_shapes=[
            pltpu.VMEM((3 * BOXES, 16, 128), BF16),
            pltpu.SMEM((BOXES, 128), jnp.int32),
            pltpu.SemaphoreType.DMA,
        ],
        compiler_params=params(),
        cost_estimate=cost(5.0),
        name="leaf",
    )(ints, su, ev, od, wl)


def run_field(ints, up, ev, x3, be, bo, wu, xv, xe, part, near):
    return pl.pallas_call(
        field_kernel,
        out_shape=shape(BOXES, 1024, dtype=F32),
        in_specs=[VM] * 11,
        out_specs=VM,
        scratch_shapes=[
            pltpu.VMEM((12 * PARENTS, 16, 128), BF16),
            pltpu.VMEM((BOXES * 16, 128), F32),
            pltpu.VMEM((8 * VP, 128), F32),
            pltpu.SMEM((8, 128), jnp.int32),
            pltpu.SemaphoreType.DMA,
        ],
        compiler_params=params(),
        cost_estimate=cost(3.0),
        name="field",
    )(ints, up, ev, x3, be, bo, wu, xv, xe, part, near)


def local(
    charges, coords, basis, transfer, leaf_table, upper_table, near_ids, near_count, leaf_ids, parent_ids
):
    flat = ("box", "sub")
    boxes = lax.axis_size("box")
    subs = lax.axis_size("sub")
    chain = boxes * subs
    ints, xv, su, up, xe = run_prepare(
        charges, coords, near_ids, near_count, leaf_ids, parent_ids, basis, transfer
    )
    ev = lax.ppermute(su, "sub", [(i, i ^ 1) for i in range(subs)])
    od = lax.ppermute(su, flat, [(i, ((i + 1) ^ 1) - 1) for i in range(1, chain - 1)])
    pair = jnp.concatenate([up, ev[UP_ROW:]], axis=0)
    x3 = lax.ppermute(pair, "sub", [(i, i ^ 3) for i in range(subs)])
    wl, wu = run_tables(leaf_table, upper_table, pair)
    tab, at = run_near_tables(su, ev, od, coords)
    part = run_leaf(ints, su, ev, od, wl)
    branch = jnp.concatenate([pair, x3], axis=0)
    be = lax.ppermute(branch, "box", [(i, i ^ 1) for i in range(boxes)])
    bo = lax.ppermute(branch, "box", [(i, ((i + 1) ^ 1) - 1) for i in range(1, boxes - 1)])
    near = run_near(ints, tab, at, x3)
    return run_field(ints, up, ev, x3, be, bo, wu, xv, xe, part, near)


def solution(mesh):
    rows = P(("box", "sub"), None)
    placed = (rows, rows, rows, rows, P(), P(), rows, P(("box", "sub")), rows, rows)
    return jax.shard_map(
        local, mesh=mesh, in_specs=placed, out_specs=P(("box", "sub"), None), check_vma=False
    )
```
